128 devices in a mesh: rows: 32 (over x, y, core), cols: 4 (over z).
Axes of the slice: x: 4, y: 4, z: 4, core: 2. Of those that a mesh axis runs over, the one named last changes fastest.
Arguments:
- latent_tokens: bfloat16 [8, 6656, 64], P(None, 'rows'), may hold values from -6 to 6
- cache_latent: bfloat16 [8, 2, 320, 112, 16], P(None, None, 'rows', 'cols'), may hold values from -6 to 6
- cache_middle: bfloat16 [8, 2, 320, 112, 384], P(None, None, 'rows', 'cols'), may hold values from -6 to 6
- entry_weight: bfloat16 [3, 3, 3, 16, 384], replicated, may hold values from -0.3125 to 0.3125
- time_weight: bfloat16 [3, 384, 768], replicated, may hold values from -0.1875 to 0.1875
- up_weight: bfloat16 [3, 3, 384, 192], replicated, may hold values from -0.109375 to 0.109375
- norm_gain: float32 [192], replicated, may hold values from 0.5 to 1.5
- row_ramp: int32 [32], replicated, may hold values from 2 to 4, as said below
- col_ramp: int32 [4], replicated, may hold values from 2 to 4, as said below
Outputs:
- blended: bfloat16 [8, 512, 208, 384], P(None, 'rows', 'cols')
The draws below stay inside these ranges and needn't reach their ends.
Inputs may be any that keep to these rules, and one draw needn't show every extreme that they name: `row_ramp`: entry t, t >= 1, is the ramp length in output cells at the boundary between tiles t - 1 and t; entry 0 is not read. `col_ramp`: entry t, t >= 1, is the ramp length in output cells at the boundary between tiles t - 1 and t; entry 0 is not read.
All inputs are finite; a program needn't handle non-finite values.
Results may differ from the reference program's by a relative error of at most 0.0054.
Values may be sent and summed in bfloat16 or wider, within the bound.
No kernel may reach another device: no remote copies, remote signals or barrier semaphores. Data moves between devices by JAX's collectives and lax.ppermute only.
A program may use at most 192 MiB of HBM per device.

```python
import jax
import jax.numpy as jnp
from jax import lax

C_LAT = 16
C_MID = 384
C_UP = 192
LR = 8
LC = 26
VIDEOS = 8
OV = 1
GRID_R = 32
GRID_C = 4
TR = 10
TC = 28
H = 256
W = 104
TOKENS = 6656


def ramp_values(key, amount):
    picked = jax.random.randint(key, (amount,), 2, 4 * OV + 1)
    order_key = jax.random.fold_in(key, 7)
    shuffled = jax.random.permutation(order_key, amount - 1) + 1
    picked = picked.at[shuffled[0]].set(4 * OV)
    picked = picked.at[shuffled[1]].set(2)
    return picked.astype(jnp.int32)


def draw_row_ramp(key, part):
    return ramp_values(jax.random.fold_in(key, 11), GRID_R)


def draw_col_ramp(key, part):
    return ramp_values(jax.random.fold_in(key, 12), GRID_C)


def shard_levels(rng, dims, shards, smallest, largest):
    factor_of, own = 1.0, jax.random.fold_in(rng, 6)
    for position, parts in shards:
        draws = jnp.exp(jax.random.uniform(jax.random.fold_in(own, position), (parts,), jnp.float32, smallest / len(shards), largest / len(shards)))
        factor_of = factor_of * jnp.repeat(draws, dims[position] // parts).reshape([-1 if axis == position else 1 for axis in range(len(dims))])
    return factor_of


def centred(rng, dims, width, limit, cuts=(), held_as=jnp.bfloat16):
    entries = jax.random.normal(rng, dims, jnp.float32) * width
    if len(cuts) > 0:
        entries = shard_levels(rng, dims, cuts, -0.22, 0.18) * entries
    return jnp.clip(entries, min=-limit, max=limit).astype(held_as)


def setup_inputs(seed: int = 0) -> dict:
    keys = jax.random.split(jax.random.key(seed), 10)
    latent_tokens = centred(keys[0], (VIDEOS, TOKENS, 4 * C_LAT), 1.0, 6.0, ((1, 32),))
    cache_latent = centred(keys[1], (VIDEOS, 2, GRID_R * TR, GRID_C * TC, C_LAT), 1.0, 6.0, ((2, 32), (3, 4)))
    cache_middle = centred(keys[2], (VIDEOS, 2, GRID_R * TR, GRID_C * TC, C_MID), 1.0, 6.0, ((2, 32), (3, 4)))
    entry_weight = centred(keys[3], (3, 3, 3, C_LAT, C_MID), (27 * C_LAT) ** -0.5, 0.3125)
    time_weight = centred(keys[4], (3, C_MID, 2 * C_MID), (3 * C_MID) ** -0.5, 0.1875)
    up_weight = centred(keys[5], (3, 3, C_MID, C_UP), (9 * C_MID) ** -0.5, 0.109375)
    norm_gain = jnp.clip(1.0 + 0.1 * jax.random.normal(keys[6], (C_UP,), jnp.float32), 0.5, 1.5)
    row_ramp = draw_row_ramp(jax.random.fold_in(keys[9], 71), 0)
    col_ramp = draw_col_ramp(jax.random.fold_in(keys[9], 71), 0)
    return {"latent_tokens": latent_tokens, "cache_latent": cache_latent, "cache_middle": cache_middle, "entry_weight": entry_weight, "time_weight": time_weight, "up_weight": up_weight, "norm_gain": norm_gain, "row_ramp": row_ramp, "col_ramp": col_ramp}


EPSILON = 1e-06

def unpatch(tokens, rows_all, width_full):
    videos_n = tokens.shape[0]
    lat_chan = tokens.shape[2] // 4
    shaped = tokens.reshape(videos_n, rows_all // 2, width_full // 2, 2, 2, lat_chan)
    shaped = jnp.transpose(shaped, (0, 1, 3, 2, 4, 5))
    return shaped.reshape(videos_n, rows_all, width_full, lat_chan)

def ramp_weight(boundary, ramp_table, amount, places, core_len):
    looked = jnp.clip(boundary, 1, amount - 1)
    length = jnp.sum(jnp.where(jnp.arange(amount, dtype=jnp.int32) == looked, ramp_table, 0)).astype(jnp.float32)
    sloped = jnp.clip((places + 0.5 - (boundary * core_len).astype(jnp.float32)) / length + 0.5, 0.0, 1.0)
    return jnp.where(boundary <= 0, 1.0, jnp.where(boundary >= amount, 0.0, sloped))

def activate(upsampled, norm_gain):
    split_up = upsampled.reshape(upsampled.shape[:-1] + (2, norm_gain.shape[0]))
    scaled = split_up * lax.rsqrt(lax.optimization_barrier(jnp.mean(split_up * split_up, axis=-1, keepdims=True)) + EPSILON) * norm_gain
    return jax.nn.silu(scaled).reshape(upsampled.shape).astype(jnp.bfloat16)

def tile_output(tile_lat, lat_cache, mid_cache, entry_weight, time_weight, up_weight, norm_gain):
    frames_in = jnp.concatenate([lat_cache, tile_lat[:, None]], axis=1).astype(jnp.float32)
    entry_out = lax.conv_general_dilated(frames_in, entry_weight.astype(jnp.float32), (1, 1, 1), ((0, 0), (1, 1), (1, 1)), dimension_numbers=('NDHWC', 'DHWIO', 'NDHWC'), precision=lax.Precision.HIGHEST, preferred_element_type=jnp.float32)
    entry_out = lax.optimization_barrier(entry_out[:, 0].astype(jnp.bfloat16))
    stacked = jnp.concatenate([mid_cache, entry_out[:, None]], axis=1).astype(jnp.float32)
    doubled = jnp.einsum('bkhwc,kco->bhwo', stacked, time_weight.astype(jnp.float32), precision=lax.Precision.HIGHEST)
    doubled = lax.optimization_barrier(doubled.astype(jnp.bfloat16))
    channels = entry_weight.shape[4]
    outputs = []
    for frame_no in range(2):
        picked = doubled[..., frame_no * channels:(frame_no + 1) * channels]
        larger = jnp.repeat(jnp.repeat(picked, 2, axis=1), 2, axis=2).astype(jnp.float32)
        outputs.append(lax.conv_general_dilated(larger, up_weight.astype(jnp.float32), (1, 1), ((1, 1), (1, 1)), dimension_numbers=('NHWC', 'HWIO', 'NHWC'), precision=lax.Precision.HIGHEST, preferred_element_type=jnp.float32))
    return activate(jnp.concatenate(outputs, axis=-1), norm_gain)

def reference(latent_tokens, cache_latent, cache_middle, entry_weight, time_weight, up_weight, norm_gain, row_ramp, col_ramp):
    latent = unpatch(latent_tokens, H, W)
    padded_lat = jnp.pad(latent, ((0, 0), (OV, OV), (OV, OV), (0, 0)))
    canvas = jnp.zeros((VIDEOS, 2 * H + 4 * OV, 2 * W + 4 * OV, 2 * C_UP), jnp.float32)
    zero_index = jnp.zeros((), jnp.int32)

    def add_tile(tile_no, canvas):
        tile_no = jnp.asarray(tile_no).astype(jnp.int32)
        row_pos = (tile_no // GRID_C).astype(jnp.int32)
        col_pos = (tile_no % GRID_C).astype(jnp.int32)
        tile_lat = lax.dynamic_slice(padded_lat, (zero_index, (row_pos * LR).astype(jnp.int32), (col_pos * LC).astype(jnp.int32), zero_index), (VIDEOS, TR, TC, C_LAT))
        lat_cache = lax.dynamic_slice(cache_latent, (zero_index, zero_index, (row_pos * TR).astype(jnp.int32), (col_pos * TC).astype(jnp.int32), zero_index), (VIDEOS, 2, TR, TC, C_LAT))
        mid_cache = lax.dynamic_slice(cache_middle, (zero_index, zero_index, (row_pos * TR).astype(jnp.int32), (col_pos * TC).astype(jnp.int32), zero_index), (VIDEOS, 2, TR, TC, C_MID))
        tile_out = tile_output(tile_lat, lat_cache, mid_cache, entry_weight, time_weight, up_weight, norm_gain)
        row_places = (2 * (row_pos * LR - OV)).astype(jnp.float32) + jnp.arange(2 * TR, dtype=jnp.float32)
        col_places = (2 * (col_pos * LC - OV)).astype(jnp.float32) + jnp.arange(2 * TC, dtype=jnp.float32)
        row_weight = ramp_weight(row_pos, row_ramp, GRID_R, row_places, 2 * LR) - ramp_weight(row_pos + 1, row_ramp, GRID_R, row_places, 2 * LR)
        col_weight = ramp_weight(col_pos, col_ramp, GRID_C, col_places, 2 * LC) - ramp_weight(col_pos + 1, col_ramp, GRID_C, col_places, 2 * LC)
        contribution = tile_out.astype(jnp.float32) * row_weight[None, :, None, None] * col_weight[None, None, :, None]
        corner = (zero_index, (2 * row_pos * LR).astype(jnp.int32), (2 * col_pos * LC).astype(jnp.int32), zero_index)
        previous = lax.dynamic_slice(canvas, corner, contribution.shape)
        return lax.dynamic_update_slice(canvas, previous + contribution, corner)
    canvas = lax.fori_loop(0, GRID_R * GRID_C, add_tile, canvas)
    return canvas[:, 2 * OV:2 * OV + 2 * H, 2 * OV:2 * OV + 2 * W].astype(jnp.bfloat16)
```

```python
import functools

import jax
import jax.numpy as jnp
from jax import lax
from jax.experimental import pallas as pl
from jax.experimental.pallas import tpu as pltpu
from jax.sharding import PartitionSpec as P

EPSILON = 1e-06
BF = jnp.bfloat16
F32 = jnp.float32
VID, C, U = 8, 384, 192
TR, TC = 10, 28
ROWS, COLS = 32, 4
NT = (((1,), (1,)), ((), ()))


def shift(value, axis, step):
    size = lax.axis_size(axis)
    pairs = [(i, i + step) for i in range(size) if 0 <= i + step < size]
    return lax.ppermute(value, axis, pairs)


def mix_body(x_ref, cm_ref, we_ref, wt_ref, d_ref, *, rows):
    g = pl.program_id(0)

    @pl.when(g == 0)
    def _():
        d_ref[...] = jnp.zeros(d_ref.shape, d_ref.dtype)

    wide = (TC + 2) * VID
    base = pl.multiple_of(g * rows * wide, 16)
    taps = jnp.concatenate([x_ref[pl.ds(base + k * wide, rows * wide), :] for k in range(3)], axis=1)
    part = jnp.dot(taps, we_ref[...], preferred_element_type=F32).reshape(rows, TC + 2, VID, 3 * C)
    entry = part[:, 0:TC, :, 0:C] + part[:, 1 : TC + 1, :, C : 2 * C] + part[:, 2 : TC + 2, :, 2 * C :]
    entry = entry.reshape(rows * TC * VID, C).astype(BF)
    stacked = jnp.concatenate([cm_ref[...], entry], axis=1)
    out = jnp.dot(stacked, wt_ref[...], preferred_element_type=F32)
    out = out.reshape(rows, TC, 1, VID, 2 * C)
    out = jnp.concatenate([out[..., :C], out[..., C:]], axis=2)
    d_ref[pl.ds(1 + g * rows, rows), 1 : TC + 1] = out.reshape(rows, TC, 2 * VID, C).astype(BF)


def mix(x, cm, we, wt):
    rows = 2
    return pl.pallas_call(
        functools.partial(mix_body, rows=rows),
        grid=(TR // rows,),
        in_specs=[
            pl.BlockSpec(x.shape, lambda g: (0, 0)),
            pl.BlockSpec((rows * TC * VID, 2 * C), lambda g: (g, 0)),
            pl.BlockSpec(we.shape, lambda g: (0, 0)),
            pl.BlockSpec(wt.shape, lambda g: (0, 0)),
        ],
        out_specs=pl.BlockSpec((TR + 2, TC + 2, 2 * VID, C), lambda g: (0, 0, 0, 0)),
        out_shape=jax.ShapeDtypeStruct((TR + 2, TC + 2, 2 * VID, C), BF),
        name="mix",
    )(x, cm, we, wt)


def fold(ut_ref, w_ref):
    def rows_of(a, kr):
        return ((0,), (1, 2)) [kr] if a == 0 else ((0, 1), (2,))[kr]

    for a in range(2):
        for b in range(2):
            for kr in range(2):
                for kc in range(2):
                    terms = [ut_ref[r, c].astype(F32) for r in rows_of(a, kr) for c in rows_of(b, kc)]
                    w = functools.reduce(jnp.add, terms).astype(BF)
                    at = (kr * 2 + kc) * C
                    w_ref[2 * a + b, 0:U, at : at + C] = w
                    w_ref[2 * a + b, U:256, at : at + C] = w[0:64]


def phase(d_ref, w_ref, gain, i0, ni, j0, nj, a, b):
    m = ni * nj * 2 * VID
    taps = [
        d_ref[pl.ds(i0 + a + kr, ni), pl.ds(j0 + b + kc, nj)].reshape(m, C)
        for kr in range(2)
        for kc in range(2)
    ]
    res = lax.dot_general(jnp.concatenate(taps, axis=1), w_ref[2 * a + b], NT, preferred_element_type=F32)
    res = res.reshape(ni * nj, 2, VID, 256)
    one = res[:, 0].reshape(ni * nj * VID, 256)
    two = res[:, 1].reshape(ni * nj * VID, 256)
    low = lax.broadcasted_iota(jnp.int32, (1, 128), 1) < 64
    o0 = one[:, :128]
    o1 = jnp.where(low, one[:, 128:], two[:, 128:])
    o2 = jnp.where(low, two[:, 128:], two[:, :128])
    q1 = o1 * o1
    s0 = jnp.sum(o0 * o0 + jnp.where(low, q1, 0.0), axis=1, keepdims=True)
    s1 = jnp.sum(o2 * o2 + jnp.where(low, 0.0, q1), axis=1, keepdims=True)
    r0 = lax.rsqrt(s0 * (1.0 / U) + EPSILON)
    r1 = lax.rsqrt(s1 * (1.0 / U) + EPSILON)
    o2 = pltpu.roll(o2, 64, 1)
    outs = []
    for k, (o, r) in enumerate(((o0, r0), (o1, jnp.where(low, r0, r1)), (o2, r1))):
        h = o * r * gain[:, 128 * k : 128 * (k + 1)]
        outs.append(h + h * jnp.tanh(h))
    return jnp.concatenate(outs, axis=1)


def both(d_ref, w_ref, gain, i0, ni, j0, nj, a):
    n = ni * nj
    outs = [phase(d_ref, w_ref, gain, i0, ni, j0, nj, a, b).reshape(n, 1, VID, 2 * U) for b in range(2)]
    return jnp.concatenate(outs, axis=1).reshape(ni, nj, 2 * VID, 2 * U).astype(BF)


def half_gain(gain_ref):
    return jnp.concatenate([gain_ref[...], gain_ref[...]], axis=1) * 0.5


def rim_body(d_ref, ut_ref, gain_ref, top_ref, low_ref, left_ref, right_ref, w_ref):
    fold(ut_ref, w_ref)
    gain = half_gain(gain_ref)
    for a in range(2):
        for j, ref in ((0, left_ref), (TC - 1, right_ref)):
            ref[:, a] = both(d_ref, w_ref, gain, 0, TR, j, 1, a)[:, 0]
        for i, ref in ((0, top_ref), (TR - 1, low_ref)):
            ref[a] = both(d_ref, w_ref, gain, i, 1, 1, TC - 2, a)[0]


def rims(d, ut, gain):
    strip = jax.ShapeDtypeStruct((2, TC - 2, 2 * VID, 2 * U), BF)
    side = jax.ShapeDtypeStruct((TR, 2, 2 * VID, 2 * U), BF)
    return pl.pallas_call(
        rim_body,
        out_shape=(strip, strip, side, side),
        scratch_shapes=[pltpu.VMEM((4, 256, 4 * C), BF)],
        name="rims",
    )(d, ut, gain)


def core_body(d_ref, ut_ref, gain_ref, o_ref, w_ref):
    i = pl.program_id(0) + 1

    @pl.when(i == 1)
    def _():
        fold(ut_ref, w_ref)

    gain = half_gain(gain_ref)
    for a in range(2):
        o_ref[a] = both(d_ref, w_ref, gain, i, 1, 1, TC - 2, a)[0]


def core(d, ut, gain):
    return pl.pallas_call(
        core_body,
        grid=(TR - 2,),
        in_specs=[
            pl.BlockSpec(d.shape, lambda g: (0, 0, 0, 0)),
            pl.BlockSpec(ut.shape, lambda g: (0, 0, 0, 0)),
            pl.BlockSpec(gain.shape, lambda g: (0, 0)),
        ],
        out_specs=pl.BlockSpec((2, TC - 2, 2 * VID, 2 * U), lambda g: (g, 0, 0, 0)),
        out_shape=jax.ShapeDtypeStruct((2 * (TR - 2), TC - 2, 2 * VID, 2 * U), BF),
        scratch_shapes=[pltpu.VMEM((4, 256, 4 * C), BF)],
        name="core",
    )(d, ut, gain)


def ramp(pos, table_ref, amount, place, length):
    step = table_ref[jnp.clip(pos, 1, amount - 1)].astype(F32)
    sloped = jnp.clip(jnp.full((1, 1), place + 0.5, F32) / jnp.full((1, 1), step, F32) + 0.5, 0.0, 1.0)
    return jnp.where(pos <= 0, 1.0, jnp.where(pos >= amount, 0.0, sloped))


def blend_body(pos_ref, rr_ref, cr_ref, a_ref, left_ref, right_ref, top_ref, low_ref, o_ref, buf):
    g = pl.program_id(0)
    r, c = pos_ref[0], pos_ref[1]
    up = [ramp(r, rr_ref, ROWS, p, 16) for p in (0, 1)]
    down = [ramp(r + 1, rr_ref, ROWS, p, 16) for p in (-2, -1)]
    n = a_ref.shape[1]
    last = pl.num_programs(0) - 1

    def finish(jj, side, w):
        for b in range(2):
            for lt in range(3):
                lanes = slice(128 * lt, 128 * (lt + 1))
                vids = slice(VID * b, VID * (b + 1))

                def across(own, other):
                    own = own.astype(F32)
                    if side is None:
                        return own
                    return own * (1.0 - w[b]) + other.astype(F32) * w[b]

                for p in range(16):
                    v = across(a_ref[p, jj, vids, lanes], None if side is None else side[1 + p // 2, p % 2, vids, lanes])
                    slot = 0 if side is left_ref else TC - 1
                    if p < 2:
                        t = across(
                            top_ref[p, 1 + n * g + jj, vids, lanes],
                            None if side is None else top_ref[p, slot, vids, lanes],
                        )
                        v = v * up[p] + t * (1.0 - up[p])
                    if p > 13:
                        t = across(
                            low_ref[p - 14, 1 + n * g + jj, vids, lanes],
                            None if side is None else low_ref[p - 14, slot, vids, lanes],
                        )
                        v = v * (1.0 - down[p - 14]) + t * down[p - 14]
                    buf[3 * b + lt, pl.ds(p, VID, stride=16), :] = v
                for v in range(VID):
                    o_ref[v, 2 * jj + b, :, lanes] = buf[3 * b + lt, 16 * v : 16 * (v + 1), :].astype(BF)

    for jj in range(n):
        if jj == 0:

            @pl.when(g == 0)
            def _():
                w = [1.0 - ramp(c, cr_ref, COLS, x, 52) for x in (0, 1)]
                finish(0, left_ref, w)

            @pl.when(g > 0)
            def _():
                finish(0, None, None)

        elif jj == n - 1:

            @pl.when(g == last)
            def _():
                w = [ramp(c + 1, cr_ref, COLS, x, 52) for x in (-2, -1)]
                finish(n - 1, right_ref, w)

            @pl.when(g < last)
            def _():
                finish(n - 1, None, None)

        else:
            finish(jj, None, None)


def blend(pos, row_ramp, col_ramp, a, left, right, top, low):
    n = 2
    smem = pl.BlockSpec(memory_space=pltpu.SMEM)
    whole = lambda v: pl.BlockSpec(v.shape, lambda g: (0,) * v.ndim)
    return pl.pallas_call(
        blend_body,
        grid=((TC - 2) // n,),
        in_specs=[
            smem,
            smem,
            smem,
            pl.BlockSpec((16, n, 2 * VID, 2 * U), lambda g: (0, g, 0, 0)),
            whole(left),
            whole(right),
            whole(top),
            whole(low),
        ],
        out_specs=pl.BlockSpec((VID, 2 * n, 16, 2 * U), lambda g: (0, g, 0, 0)),
        out_shape=jax.ShapeDtypeStruct((VID, 52, 16, 2 * U), BF),
        scratch_shapes=[pltpu.VMEM((6, 16 * VID, 128), F32)],
        name="blend",
    )(pos, row_ramp, col_ramp, a, left, right, top, low)


def prepare(tokens, cache_latent, cache_middle, entry_weight, time_weight, up_weight, norm_gain, col_pos, halo=True):
    small = tokens.reshape(VID, 4, 52, 64)
    small = jnp.pad(small, ((0, 0), (0, 0), (1, 1), (0, 0)))
    small = lax.dynamic_slice_in_dim(small, col_pos * 13, 15, axis=2)
    if halo:
        before = shift(small[:, 3:], "rows", 1)
        after = shift(small[:, :1], "rows", -1)
    else:
        before, after = jnp.zeros_like(small[:, 3:]), jnp.zeros_like(small[:, 3:])
    small = jnp.concatenate([before, small, after], axis=1).reshape(VID, 6, 15, 2, 2, 16)
    lat = jnp.transpose(small, (1, 3, 2, 4, 0, 5)).reshape(12, 30, VID, 16)[1:11, 1:29]
    cached = jnp.transpose(cache_latent, (2, 3, 0, 1, 4)).reshape(TR, TC, VID, 32)
    x = jnp.pad(jnp.concatenate([cached, lat], axis=3), ((1, 1), (1, 1), (0, 0), (0, 0)))
    x = x.reshape(12 * 30 * VID, 48)
    cm = jnp.transpose(cache_middle, (2, 3, 0, 1, 4)).reshape(TR * TC * VID, 2 * C)
    we = jnp.transpose(entry_weight, (1, 0, 3, 2, 4)).reshape(144, 3 * C)
    wt = time_weight.reshape(3 * C, 2 * C)
    ut = jnp.transpose(up_weight, (0, 1, 3, 2))
    gain = norm_gain.reshape(1, U)
    return x, cm, we, wt, ut, gain


def per_device(
    latent_tokens,
    cache_latent,
    cache_middle,
    entry_weight,
    time_weight,
    up_weight,
    norm_gain,
    row_ramp,
    col_ramp,
):
    row_pos = lax.axis_index("rows")
    col_pos = lax.axis_index("cols")
    x, cm, we, wt, ut, gain = prepare(
        latent_tokens, cache_latent, cache_middle, entry_weight, time_weight, up_weight, norm_gain, col_pos
    )
    d = mix(x, cm, we, wt)
    top, low, left, right = rims(d, ut, gain)
    from_left = shift(right, "cols", 1)
    from_right = shift(left, "cols", -1)

    def widen(strip, i):
        return jnp.concatenate([from_left[i][:, None], strip, from_right[i][:, None]], axis=1)

    from_above = shift(widen(low, TR - 1), "rows", 1)
    from_below = shift(widen(top, 0), "rows", -1)
    a = core(d, ut, gain)
    pos = jnp.stack([row_pos, col_pos]).astype(jnp.int32)
    out = blend(pos, row_ramp, col_ramp, a, from_left, from_right, from_above, from_below)
    return jnp.transpose(out, (0, 2, 1, 3))


def solution(mesh):
    in_specs = (
        P(None, "rows", None),
        P(None, None, "rows", "cols", None),
        P(None, None, "rows", "cols", None),
        P(),
        P(),
        P(),
        P(),
        P(),
        P(),
    )
    out_specs = P(None, "rows", "cols", None)
    return jax.shard_map(
        per_device, mesh=mesh, in_specs=in_specs, out_specs=out_specs, check_vma=False
    )
```

```python
import functools

import jax
import jax.numpy as jnp
from jax import lax
from jax.experimental import pallas as pl
from jax.experimental.pallas import tpu as pltpu
from jax.sharding import PartitionSpec as P

EPSILON = 1e-06
BF = jnp.bfloat16
F32 = jnp.float32
VID, C, U = 8, 384, 192
TR, TC = 10, 28
ROWS, COLS = 32, 4
NT = (((1,), (1,)), ((), ()))


def shift(value, axis, step):
    size = lax.axis_size(axis)
    pairs = [(i, i + step) for i in range(size) if 0 <= i + step < size]
    return lax.ppermute(value, axis, pairs)


VM = pl.BlockSpec(memory_space=pltpu.VMEM)
LIMIT = pltpu.CompilerParams(vmem_limit_bytes=24 << 20)


def held(value):
    return pltpu.with_memory_space_constraint(value, pltpu.VMEM)


def call(body, name, outs, args, flops, scratch=(), out_specs=None, smem=0):
    specs = [pl.BlockSpec(memory_space=pltpu.SMEM)] * smem + [VM] * (len(args) - smem)
    args = list(args[:smem]) + [held(v) for v in args[smem:]]
    return pl.pallas_call(
        body,
        in_specs=specs,
        out_specs=jax.tree.map(lambda _: VM, outs) if out_specs is None else out_specs,
        out_shape=outs,
        scratch_shapes=list(scratch),
        compiler_params=LIMIT,
        cost_estimate=pl.CostEstimate(flops=flops, bytes_accessed=1 << 16, transcendentals=0),
        name=name,
    )(*args)


WIDE = (TC + 2) * VID
PITCH = 56
STEPS = 5


def gather_body(col, tok_ref, before_ref, after_ref, cache_ref, x_ref, t_ref, lat_ref, old_ref):
    lat_ref[...] = jnp.zeros(lat_ref.shape, F32)
    old_ref[...] = jnp.zeros(old_ref.shape, F32)
    t_ref[...] = jnp.zeros(t_ref.shape, F32)
    for v in range(VID):
        own = jnp.transpose(tok_ref[v].astype(F32))
        rows = [jnp.transpose(before_ref[v].astype(F32))]
        rows += [own[52 * i : 52 * (i + 1)] for i in range(4)]
        rows += [jnp.transpose(after_ref[v].astype(F32))]
        for i in range(6):
            t_ref[v % 2, pl.ds(i * PITCH + 1, 52), 0:64] = rows[i]
        for i in range(6):
            near = t_ref[v % 2, pl.ds(i * PITCH + 13 * col, 15), :]
            for q in range(2):
                e = 2 * i + q
                if e in (0, 11):
                    continue
                for k in range(2):
                    part = pltpu.roll(near, (32 - (2 * q + k) * 16) % 128, 1)
                    part = part[1:15] if k == 0 else part[0:14]
                    first = 2 if k == 0 else 1
                    lat_ref[pl.ds((e * (TC + 2) + first) * VID + v, 14, stride=2 * VID), :] = part
        for t in range(TR):
            both = jnp.concatenate([cache_ref[v, 0, t], cache_ref[v, 1, t]], axis=0).astype(F32)
            both = jnp.concatenate([both, jnp.zeros((96, TC), F32)], axis=0)
            old_ref[pl.ds(((t + 1) * (TC + 2) + 1) * VID + v, TC, stride=VID), :] = jnp.transpose(both)
    lane = lax.broadcasted_iota(jnp.int32, (1, 128), 1)
    x_ref[...] = jnp.where(lane < 32, old_ref[...], jnp.where(lane < 48, lat_ref[...], 0.0)).astype(BF)


def mix_body(
    pos_ref,
    tok_ref,
    before_ref,
    after_ref,
    cache_ref,
    ew_ref,
    cm_hbm,
    wt_hbm,
    d_ref,
    x_ref,
    t_ref,
    lat_ref,
    old_ref,
    we_ref,
    cm_ref,
    wt_ref,
    sem,
):
    rows = TR // STEPS
    m = rows * TC * VID
    loads = [
        pltpu.make_async_copy(cm_hbm.at[pl.ds(g * m, m)], cm_ref.at[pl.ds(g * m, m)], sem.at[g]) for g in range(STEPS)
    ]
    load_wt = pltpu.make_async_copy(wt_hbm, wt_ref, sem.at[STEPS])
    loads[0].start()
    load_wt.start()
    for load in loads[1:]:
        load.start()
    edge = jnp.zeros((TR + 2, 1, 2 * VID, C), BF)
    d_ref[:, 0:1] = edge
    d_ref[:, TC + 1 : TC + 2] = edge
    line = jnp.zeros((1, TC + 2, 2 * VID, C), BF)
    d_ref[0:1] = line
    d_ref[TR + 1 : TR + 2] = line
    for f in range(3):
        for kr in range(3):
            for kc in range(3):
                at = (kr * 3 + f) * 16
                we_ref[at : at + 16, kc * C : (kc + 1) * C] = ew_ref[f, kr, kc]
    gather_body(pos_ref[1], tok_ref, before_ref, after_ref, cache_ref, x_ref, t_ref, lat_ref, old_ref)
    for g in range(STEPS):
        base = g * rows * WIDE
        taps = [x_ref[base + k * WIDE : base + (k + rows) * WIDE, 0:48] for k in range(3)]
        part = jnp.dot(jnp.concatenate(taps, axis=1), we_ref[...], preferred_element_type=F32)
        part = part.reshape(rows, TC + 2, VID, 3 * C)
        entry = part[:, 0:TC, :, 0:C] + part[:, 1 : TC + 1, :, C : 2 * C] + part[:, 2 : TC + 2, :, 2 * C :]
        entry = entry.reshape(m, C).astype(BF)
        if g == 0:
            load_wt.wait()
        loads[g].wait()
        stacked = jnp.concatenate([cm_ref[g * m : (g + 1) * m, :], entry], axis=1)
        out = jnp.dot(stacked, wt_ref[...], preferred_element_type=F32)
        out = out.reshape(rows, TC, 1, VID, 2 * C)
        out = jnp.concatenate([out[..., :C], out[..., C:]], axis=2)
        d_ref[1 + g * rows : 1 + (g + 1) * rows, 1 : TC + 1] = out.reshape(rows, TC, 2 * VID, C).astype(BF)


def mix(pos, tok, before, after, cache, ew, cm, wt):
    args = [held(v) for v in (tok, before, after, cache, ew)]
    hbm = pl.BlockSpec(memory_space=pltpu.HBM)
    return pl.pallas_call(
        mix_body,
        in_specs=[pl.BlockSpec(memory_space=pltpu.SMEM)] + [VM] * len(args) + [hbm, hbm],
        out_specs=VM,
        out_shape=pltpu.VMEM((TR + 2, TC + 2, 2 * VID, C), BF),
        scratch_shapes=[
            pltpu.VMEM((12 * WIDE, 128), BF),
            pltpu.VMEM((2, 6 * PITCH + 8, 128), F32),
            pltpu.VMEM((12 * WIDE, 128), F32),
            pltpu.VMEM((12 * WIDE, 128), F32),
            pltpu.VMEM((144, 3 * C), BF),
            pltpu.VMEM((TR * TC * VID, 2 * C), BF),
            pltpu.VMEM((3 * C, 2 * C), BF),
            pltpu.SemaphoreType.DMA((STEPS + 1,)),
        ],
        compiler_params=LIMIT,
        cost_estimate=pl.CostEstimate(flops=2 * 60000 * 65536, bytes_accessed=1 << 16, transcendentals=0),
        name="mix",
    )(pos, *args, cm, wt)


def fold_body(ut_ref, w_ref):
    def sums(get):
        return (get(0), get(1) + get(2)), (get(0) + get(1), get(2))

    rows = [sums(lambda r: ut_ref[r, c].astype(F32)) for c in range(3)]
    for a in range(2):
        for kr in range(2):
            cols = sums(lambda c: rows[c][a][kr])
            for b in range(2):
                for kc in range(2):
                    w = cols[b][kc].astype(BF)
                    at = (kr * 2 + kc) * C
                    w_ref[2 * a + b, 0:U, at : at + C] = w
                    w_ref[2 * a + b, U:256, at : at + C] = w[0:64]


def fold(ut):
    return call(fold_body, "fold", pltpu.VMEM((4, 256, 4 * C), BF), (ut,), 1 << 24)


def phase(d_ref, w_ref, gain, areas, a, b):
    parts, cells = [], 0
    for i0, ni, j0, nj in areas:
        taps = [
            d_ref[i0 + a + kr : i0 + a + kr + ni, j0 + b + kc : j0 + b + kc + nj].reshape(ni * nj * 2 * VID, C)
            for kr in range(2)
            for kc in range(2)
        ]
        parts.append(jnp.concatenate(taps, axis=1))
        cells += ni * nj
    full = jnp.concatenate(parts, axis=0) if len(parts) > 1 else parts[0]
    res = lax.dot_general(full, w_ref[2 * a + b], NT, preferred_element_type=F32)
    res = res.reshape(cells, 2, VID, 256)
    one = res[:, 0].reshape(cells * VID, 256)
    two = res[:, 1].reshape(cells * VID, 256)
    low = lax.broadcasted_iota(jnp.int32, (1, 128), 1) < 64
    o0 = one[:, :128]
    o1 = jnp.where(low, one[:, 128:], two[:, 128:])
    o2 = jnp.where(low, two[:, 128:], two[:, :128])
    q1 = o1 * o1
    s0 = jnp.sum(o0 * o0 + jnp.where(low, q1, 0.0), axis=1, keepdims=True)
    s1 = jnp.sum(o2 * o2 + jnp.where(low, 0.0, q1), axis=1, keepdims=True)
    r0 = lax.rsqrt(s0 * (1.0 / U) + EPSILON)
    r1 = lax.rsqrt(s1 * (1.0 / U) + EPSILON)
    o2 = pltpu.roll(o2, 64, 1)
    outs = []
    for k, (o, r) in enumerate(((o0, r0), (o1, jnp.where(low, r0, r1)), (o2, r1))):
        h = o * r * gain[:, 128 * k : 128 * (k + 1)]
        outs.append(h + h * jnp.tanh(h))
    return jnp.concatenate(outs, axis=1)


def both(d_ref, w_ref, gain, areas, a):
    n = sum(area[1] * area[3] for area in areas)
    outs = [phase(d_ref, w_ref, gain, areas, a, b).reshape(n, 1, VID, 2 * U) for b in range(2)]
    return jnp.concatenate(outs, axis=1).reshape(n, 2 * VID, 2 * U).astype(BF)


def half_gain(gain_ref):
    return jnp.concatenate([gain_ref[...], gain_ref[...]], axis=1) * 0.5


def sides_body(d_ref, w_ref, gain_ref, left_ref, right_ref):
    gain = half_gain(gain_ref)
    for a in range(2):
        v = both(d_ref, w_ref, gain, ((0, TR, 0, 1), (0, TR, TC - 1, 1)), a)
        left_ref[:, a] = v[:TR]
        right_ref[:, a] = v[TR:]


def sides(d, w, gain):
    side = jax.ShapeDtypeStruct((TR, 2, 2 * VID, 2 * U), BF)
    return call(sides_body, "sides", (side, side), (d, w, gain), 2 * 320 * 24 * 65536)


def strips_body(d_ref, w_ref, gain_ref, fl_ref, fr_ref, done_ref, top_ref, low_ref):
    del done_ref
    gain = half_gain(gain_ref)
    n = TC - 2
    for a in range(2):
        v = both(d_ref, w_ref, gain, ((0, 1, 1, n), (TR - 1, 1, 1, n)), a)
        top_ref[a, 1 : n + 1] = v[:n]
        low_ref[a, 1 : n + 1] = v[n:]
        for ref, i in ((top_ref, 0), (low_ref, TR - 1)):
            ref[a, 0] = fl_ref[i, a]
            ref[a, n + 1] = fr_ref[i, a]


def strips(d, w, gain, fl, fr, done):
    strip = jax.ShapeDtypeStruct((2, TC, 2 * VID, 2 * U), BF)
    return call(strips_body, "strips", (strip, strip), (d, w, gain, fl, fr, done), 2 * 832 * 24 * 65536)


FIRST, SPLIT = 3, 7


def upper_body(d_ref, w_ref, gain_ref, o_ref, *, start, stop):
    gain = half_gain(gain_ref)
    for i in range(start, stop):
        for a in range(2):
            o_ref[2 * (i - start) + a] = both(d_ref, w_ref, gain, ((i + 1, 1, 1, TC - 2),), a)


def upper(d, w, gain, start, stop):
    out = pltpu.VMEM((2 * (stop - start), TC - 2, 2 * VID, 2 * U), BF)
    body = functools.partial(upper_body, start=start, stop=stop)
    return call(body, "upper%d" % start, out, (d, w, gain), 2 * (stop - start) * 416 * 24 * 65536)


def ramp(pos, table_ref, amount, place):
    step = table_ref[jnp.clip(pos, 1, amount - 1)].astype(F32)
    sloped = jnp.clip(jnp.full((1, 1), place + 0.5, F32) / jnp.full((1, 1), step, F32) + 0.5, 0.0, 1.0)
    return jnp.where(pos <= 0, 1.0, jnp.where(pos >= amount, 0.0, sloped))


GROUP = 2


def lower_body(
    pos_ref, rr_ref, cr_ref, d_ref, w_ref, gain_ref, u_ref, v_ref, fl_ref, fr_ref, top_ref, low_ref, o_ref, a_ref, buf, sem
):
    gain = half_gain(gain_ref)
    for i in range(1 + SPLIT, TR - 1):
        for a in range(2):
            a_ref[2 * (i - 1 - SPLIT) + a] = both(d_ref, w_ref, gain, ((i, 1, 1, TC - 2),), a)
    r, c = pos_ref[0], pos_ref[1]
    up = [ramp(r, rr_ref, ROWS, p) for p in (0, 1)]
    down = [ramp(r + 1, rr_ref, ROWS, p) for p in (-2, -1)]
    groups = (TC - 2) // GROUP

    def sends(g):
        at = pl.ds(g * 2 * GROUP, 2 * GROUP)
        return pltpu.make_async_copy(buf.at[:, at], o_ref.at[:, at], sem.at[g])

    def put(j, rows):
        v = jnp.swapaxes(rows, 0, 1)
        for b in range(2):
            buf[:, 2 * j + b] = v[VID * b : VID * (b + 1)]

    def rows_of(j, k):
        if k < 2 * FIRST:
            return u_ref[k, j]
        return v_ref[k - 2 * FIRST, j] if k < 2 * SPLIT else a_ref[k - 2 * SPLIT, j]

    def inner(j):
        rows = []
        for p in range(16):
            v = rows_of(j, p)
            if p < 2:
                v = (v.astype(F32) * up[p] + top_ref[p, j + 1].astype(F32) * (1.0 - up[p])).astype(BF)
            elif p > 13:
                w = down[p - 14]
                v = (v.astype(F32) * (1.0 - w) + low_ref[p - 14, j + 1].astype(F32) * w).astype(BF)
            rows.append(v[None])
        put(j, jnp.concatenate(rows, axis=0))

    def outer(j, side_ref, slot, w):
        first = lax.broadcasted_iota(jnp.int32, (2 * VID, 1), 0) < VID
        w = jnp.where(first, w[0], w[1])

        def across(own, other):
            return own.astype(F32) * (1.0 - w) + other.astype(F32) * w

        rows = []
        for p in range(16):
            v = across(rows_of(j, p), side_ref[1 + p // 2, p % 2])
            if p < 2:
                v = v * up[p] + across(top_ref[p, j + 1], top_ref[p, slot]) * (1.0 - up[p])
            elif p > 13:
                k = down[p - 14]
                v = v * (1.0 - k) + across(low_ref[p - 14, j + 1], low_ref[p - 14, slot]) * k
            rows.append(v.astype(BF)[None])
        put(j, jnp.concatenate(rows, axis=0))

    outer(0, fl_ref, 0, [1.0 - ramp(c, cr_ref, COLS, x) for x in (0, 1)])
    for j in range(1, GROUP):
        inner(j)
    sends(0).start()

    def step(g, carry):
        for j in range(GROUP):
            inner(g * GROUP + j)
        sends(g).start()
        return carry

    lax.fori_loop(1, groups - 1, step, 0)
    for j in range(TC - 2 - GROUP, TC - 3):
        inner(j)
    outer(TC - 3, fr_ref, TC - 1, [ramp(c + 1, cr_ref, COLS, x) for x in (-2, -1)])
    sends(groups - 1).start()
    for g in range(groups):
        sends(g).wait()


def lower(pos, row_ramp, col_ramp, d, w, gain, u, v, fl, fr, top, low):
    out = jax.ShapeDtypeStruct((VID, 2 * (TC - 2), 16, 2 * U), BF)
    n = TR - 2 - SPLIT
    return call(
        lower_body,
        "lower",
        out,
        (pos, row_ramp, col_ramp, d, w, gain, u, v, fl, fr, top, low),
        2 * n * 416 * 24 * 65536,
        scratch=[
            pltpu.VMEM((2 * n, TC - 2, 2 * VID, 2 * U), BF),
            pltpu.VMEM((VID, 2 * (TC - 2), 16, 2 * U), BF),
            pltpu.SemaphoreType.DMA(((TC - 2) // GROUP,)),
        ],
        out_specs=pl.BlockSpec(memory_space=pltpu.HBM),
        smem=3,
    )


def per_device(
    latent_tokens,
    cache_latent,
    cache_middle,
    entry_weight,
    time_weight,
    up_weight,
    norm_gain,
    row_ramp,
    col_ramp,
):
    row_pos = lax.axis_index("rows")
    col_pos = lax.axis_index("cols")
    tok = jnp.transpose(latent_tokens, (0, 2, 1))
    before = shift(tok[:, :, 156:], "rows", 1)
    after = shift(tok[:, :, :52], "rows", -1)
    cache = jnp.transpose(cache_latent, (0, 1, 2, 4, 3))
    cm = jnp.transpose(cache_middle, (2, 3, 0, 1, 4)).reshape(TR * TC * VID, 2 * C)
    wt = time_weight.reshape(3 * C, 2 * C)
    ut = jnp.transpose(up_weight, (0, 1, 3, 2))
    gain = norm_gain.reshape(1, U)
    pos = jnp.stack([row_pos, col_pos]).astype(jnp.int32)
    w = fold(ut)
    d = mix(pos, tok, before, after, cache, entry_weight, cm, wt)
    left, right = sides(d, w, gain)
    from_left = shift(right, "cols", 1)
    from_right = shift(left, "cols", -1)
    u = upper(d, w, gain, 0, FIRST)
    top, low = strips(d, w, gain, from_left, from_right, u)
    from_above = shift(low, "rows", 1)
    from_below = shift(top, "rows", -1)
    v = upper(d, w, gain, FIRST, SPLIT)
    out = lower(pos, row_ramp, col_ramp, d, w, gain, u, v, from_left, from_right, from_above, from_below)
    return jnp.transpose(out, (0, 2, 1, 3))


def solution(mesh):
    in_specs = (
        P(None, "rows", None),
        P(None, None, "rows", "cols", None),
        P(None, None, "rows", "cols", None),
        P(),
        P(),
        P(),
        P(),
        P(),
        P(),
    )
    out_specs = P(None, "rows", "cols", None)
    return jax.shard_map(
        per_device, mesh=mesh, in_specs=in_specs, out_specs=out_specs, check_vma=False
    )
```

```python
import functools

import jax
import jax.numpy as jnp
from jax import lax
from jax.experimental import pallas as pl
from jax.experimental.pallas import tpu as pltpu
from jax.sharding import PartitionSpec as P

EPSILON = 1e-06
BF = jnp.bfloat16
F32 = jnp.float32
VID, C, U = 8, 384, 192
TR, TC = 10, 28
ROWS, COLS = 32, 4
NT = (((1,), (1,)), ((), ()))


def shift(value, axis, step):
    size = lax.axis_size(axis)
    pairs = [(i, i + step) for i in range(size) if 0 <= i + step < size]
    return lax.ppermute(value, axis, pairs)


VM = pl.BlockSpec(memory_space=pltpu.VMEM)
LIMIT = pltpu.CompilerParams(vmem_limit_bytes=24 << 20)


def held(value):
    return pltpu.with_memory_space_constraint(value, pltpu.VMEM)


def call(body, name, outs, args, flops, scratch=(), out_specs=None, smem=0):
    specs = [pl.BlockSpec(memory_space=pltpu.SMEM)] * smem + [VM] * (len(args) - smem)
    args = list(args[:smem]) + [held(v) for v in args[smem:]]
    return pl.pallas_call(
        body,
        in_specs=specs,
        out_specs=jax.tree.map(lambda _: VM, outs) if out_specs is None else out_specs,
        out_shape=outs,
        scratch_shapes=list(scratch),
        compiler_params=LIMIT,
        cost_estimate=pl.CostEstimate(flops=flops, bytes_accessed=1 << 16, transcendentals=0),
        name=name,
    )(*args)


WIDE = (TC + 2) * VID
PITCH = 56
STEPS = 5


def gather_body(col, tok_ref, before_ref, after_ref, cache_ref, x_ref, t_ref, lat_ref, old_ref):
    lat_ref[...] = jnp.zeros(lat_ref.shape, F32)
    old_ref[...] = jnp.zeros(old_ref.shape, F32)
    t_ref[...] = jnp.zeros(t_ref.shape, F32)
    for v in range(VID):
        own = jnp.transpose(tok_ref[v].astype(F32))
        rows = [jnp.transpose(before_ref[v].astype(F32))]
        rows += [own[52 * i : 52 * (i + 1)] for i in range(4)]
        rows += [jnp.transpose(after_ref[v].astype(F32))]
        for i in range(6):
            t_ref[v % 2, pl.ds(i * PITCH + 1, 52), 0:64] = rows[i]
        for i in range(6):
            near = t_ref[v % 2, pl.ds(i * PITCH + 13 * col, 15), :]
            for q in range(2):
                e = 2 * i + q
                if e in (0, 11):
                    continue
                for k in range(2):
                    part = pltpu.roll(near, (32 - (2 * q + k) * 16) % 128, 1)
                    part = part[1:15] if k == 0 else part[0:14]
                    first = 2 if k == 0 else 1
                    lat_ref[pl.ds((e * (TC + 2) + first) * VID + v, 14, stride=2 * VID), :] = part
        for t in range(TR):
            both = jnp.concatenate([cache_ref[v, 0, t], cache_ref[v, 1, t]], axis=0).astype(F32)
            both = jnp.concatenate([both, jnp.zeros((96, TC), F32)], axis=0)
            old_ref[pl.ds(((t + 1) * (TC + 2) + 1) * VID + v, TC, stride=VID), :] = jnp.transpose(both)
    lane = lax.broadcasted_iota(jnp.int32, (1, 128), 1)
    x_ref[...] = jnp.where(lane < 32, old_ref[...], jnp.where(lane < 48, lat_ref[...], 0.0)).astype(BF)


def mixed(x_ref, we_ref, cm_ref, wt_ref, areas):
    taps, olds, sizes = [], [], []
    for r0, nr, c0, nc in areas:
        for t in range(r0, r0 + nr):
            wide = (nc + 2) * VID
            at = [(t + k) * WIDE + c0 * VID for k in range(3)]
            taps.append(jnp.concatenate([x_ref[p : p + wide, 0:48] for p in at], axis=1))
            p = (t * TC + c0) * VID
            olds.append(cm_ref[p : p + nc * VID, :])
            sizes.append(nc)
    part = jnp.dot(jnp.concatenate(taps, axis=0), we_ref[...], preferred_element_type=F32)
    part = part.reshape(-1, VID, 3 * C)
    entry, at = [], 0
    for nc in sizes:
        three = [part[at + k : at + k + nc, :, k * C : (k + 1) * C] for k in range(3)]
        entry.append(three[0] + three[1] + three[2])
        at += nc + 2
    cells = sum(sizes)
    entry = jnp.concatenate(entry, axis=0).reshape(cells * VID, C).astype(BF)
    stacked = jnp.concatenate([jnp.concatenate(olds, axis=0), entry], axis=1)
    out = jnp.dot(stacked, wt_ref[...], preferred_element_type=F32).reshape(cells, 1, VID, 2 * C)
    out = jnp.concatenate([out[..., :C], out[..., C:]], axis=1)
    return out.reshape(cells, 2 * VID, C).astype(BF)


def edge_body(
    pos_ref,
    tok_ref,
    before_ref,
    after_ref,
    cache_ref,
    ew_ref,
    cm_ref,
    wt_ref,
    w_ref,
    gain_ref,
    x_ref,
    we_ref,
    dl_ref,
    dr_ref,
    left_ref,
    right_ref,
    t_ref,
    lat_ref,
    old_ref,
):
    dl_ref[...] = jnp.zeros(dl_ref.shape, BF)
    dr_ref[...] = jnp.zeros(dr_ref.shape, BF)
    for f in range(3):
        for kr in range(3):
            for kc in range(3):
                at = (kr * 3 + f) * 16
                we_ref[at : at + 16, kc * C : (kc + 1) * C] = ew_ref[f, kr, kc]
    gather_body(pos_ref[1], tok_ref, before_ref, after_ref, cache_ref, x_ref, t_ref, lat_ref, old_ref)
    d = mixed(x_ref, we_ref, cm_ref, wt_ref, ((0, TR, 0, 2), (0, TR, TC - 2, 2)))
    dl_ref[1 : TR + 1, 1:3] = d[: 2 * TR].reshape(TR, 2, 2 * VID, C)
    dr_ref[1 : TR + 1, 0:2] = d[2 * TR :].reshape(TR, 2, 2 * VID, C)
    gain = half_gain(gain_ref)
    for a in range(2):
        v = both(w_ref, gain, ((dl_ref, 0, TR, 0, 1), (dr_ref, 0, TR, 0, 1)), a)
        left_ref[:, a] = v[:TR]
        right_ref[:, a] = v[TR:]


def edge(pos, tok, before, after, cache, ew, cm, wt, w, gain):
    part = pltpu.VMEM((TR + 2, 3, 2 * VID, C), BF)
    side = jax.ShapeDtypeStruct((TR, 2, 2 * VID, 2 * U), BF)
    outs = (pltpu.VMEM((12 * WIDE, 128), BF), pltpu.VMEM((144, 3 * C), BF), part, part, side, side)
    return call(
        edge_body,
        "edge",
        outs,
        (pos, tok, before, after, cache, ew, cm, wt, w, gain),
        2 * 40000 * 65536,
        scratch=[
            pltpu.VMEM((2, 6 * PITCH + 8, 128), F32),
            pltpu.VMEM((12 * WIDE, 128), F32),
            pltpu.VMEM((12 * WIDE, 128), F32),
        ],
        smem=1,
    )


def rest_body(x_ref, we_ref, cm_ref, wt_ref, dl_ref, dr_ref, d_ref):
    n = TC - 4
    line = jnp.zeros((1, n, 2 * VID, C), BF)
    d_ref[0:1, 3 : n + 3] = line
    d_ref[TR + 1 : TR + 2, 3 : n + 3] = line
    d_ref[:, 0:3] = dl_ref[...]
    d_ref[:, n + 3 : n + 6] = dr_ref[...]
    rows = TR // STEPS
    for g in range(STEPS):
        d = mixed(x_ref, we_ref, cm_ref, wt_ref, ((g * rows, rows, 2, n),))
        d_ref[1 + g * rows : 1 + (g + 1) * rows, 3 : n + 3] = d.reshape(rows, n, 2 * VID, C)


def rest(x, we, cm, wt, dl, dr):
    out = pltpu.VMEM((TR + 2, TC + 2, 2 * VID, C), BF)
    return call(rest_body, "rest", out, (x, we, cm, wt, dl, dr), 2 * 45000 * 65536)


def fold_body(ut_ref, w_ref):
    def sums(get):
        return (get(0), get(1) + get(2)), (get(0) + get(1), get(2))

    rows = [sums(lambda r: ut_ref[r, c].astype(F32)) for c in range(3)]
    for a in range(2):
        for kr in range(2):
            cols = sums(lambda c: rows[c][a][kr])
            for b in range(2):
                for kc in range(2):
                    w = cols[b][kc].astype(BF)
                    at = (kr * 2 + kc) * C
                    w_ref[2 * a + b, 0:U, at : at + C] = w
                    w_ref[2 * a + b, U:256, at : at + C] = w[0:64]


def fold(ut):
    return call(fold_body, "fold", pltpu.VMEM((4, 256, 4 * C), BF), (ut,), 1 << 24)


def phase(w_ref, gain, areas, a, b):
    parts, cells = [], 0
    for d_ref, i0, ni, j0, nj in areas:
        taps = [
            d_ref[i0 + a + kr : i0 + a + kr + ni, j0 + b + kc : j0 + b + kc + nj].reshape(ni * nj * 2 * VID, C)
            for kr in range(2)
            for kc in range(2)
        ]
        parts.append(jnp.concatenate(taps, axis=1))
        cells += ni * nj
    full = jnp.concatenate(parts, axis=0) if len(parts) > 1 else parts[0]
    res = lax.dot_general(full, w_ref[2 * a + b], NT, preferred_element_type=F32)
    res = res.reshape(cells, 2, VID, 256)
    one = res[:, 0].reshape(cells * VID, 256)
    two = res[:, 1].reshape(cells * VID, 256)
    low = lax.broadcasted_iota(jnp.int32, (1, 128), 1) < 64
    o0 = one[:, :128]
    o1 = jnp.where(low, one[:, 128:], two[:, 128:])
    o2 = jnp.where(low, two[:, 128:], two[:, :128])
    q1 = o1 * o1
    s0 = jnp.sum(o0 * o0 + jnp.where(low, q1, 0.0), axis=1, keepdims=True)
    s1 = jnp.sum(o2 * o2 + jnp.where(low, 0.0, q1), axis=1, keepdims=True)
    r0 = lax.rsqrt(s0 * (1.0 / U) + EPSILON)
    r1 = lax.rsqrt(s1 * (1.0 / U) + EPSILON)
    o2 = pltpu.roll(o2, 64, 1)
    outs = []
    for k, (o, r) in enumerate(((o0, r0), (o1, jnp.where(low, r0, r1)), (o2, r1))):
        h = o * r * gain[:, 128 * k : 128 * (k + 1)]
        outs.append(h + h * jnp.tanh(h))
    return jnp.concatenate(outs, axis=1)


def both(w_ref, gain, areas, a):
    n = sum(area[2] * area[4] for area in areas)
    outs = [phase(w_ref, gain, areas, a, b).reshape(n, 1, VID, 2 * U) for b in range(2)]
    return jnp.concatenate(outs, axis=1).reshape(n, 2 * VID, 2 * U).astype(BF)


def half_gain(gain_ref):
    return jnp.concatenate([gain_ref[...], gain_ref[...]], axis=1) * 0.5


def strips_body(d_ref, w_ref, gain_ref, top_ref, low_ref):
    gain = half_gain(gain_ref)
    n = TC - 2
    for a in range(2):
        v = both(w_ref, gain, ((d_ref, 0, 1, 1, n), (d_ref, TR - 1, 1, 1, n)), a)
        top_ref[a] = v[:n]
        low_ref[a] = v[n:]


def strips(d, w, gain):
    strip = pltpu.VMEM((2, TC - 2, 2 * VID, 2 * U), BF)
    return call(strips_body, "strips", (strip, strip), (d, w, gain), 2 * 832 * 24 * 65536)


def join_body(t_ref, l_ref, fl_ref, fr_ref, top_ref, low_ref):
    n = TC - 2
    for ref, own_ref, i in ((top_ref, t_ref, 0), (low_ref, l_ref, TR - 1)):
        ref[:, 1 : n + 1] = own_ref[...]
        for a in range(2):
            ref[a, 0] = fl_ref[i, a]
            ref[a, n + 1] = fr_ref[i, a]


def join(t, l, fl, fr):
    strip = jax.ShapeDtypeStruct((2, TC, 2 * VID, 2 * U), BF)
    return call(join_body, "join", (strip, strip), (t, l, fl, fr), 1 << 20)


def upper_body(d_ref, w_ref, gain_ref, after_ref, o_ref):
    del after_ref
    gain = half_gain(gain_ref)
    for i in range(TR - 2):
        for a in range(2):
            o_ref[2 * i + a] = both(w_ref, gain, ((d_ref, i + 1, 1, 1, TC - 2),), a)


def upper(d, w, gain, after):
    out = pltpu.VMEM((2 * (TR - 2), TC - 2, 2 * VID, 2 * U), BF)
    return call(upper_body, "upper", out, (d, w, gain, after), 2 * (TR - 2) * 416 * 24 * 65536)


def ramp(pos, table_ref, amount, place):
    step = table_ref[jnp.clip(pos, 1, amount - 1)].astype(F32)
    sloped = jnp.clip(jnp.full((1, 1), place + 0.5, F32) / jnp.full((1, 1), step, F32) + 0.5, 0.0, 1.0)
    return jnp.where(pos <= 0, 1.0, jnp.where(pos >= amount, 0.0, sloped))


GROUP = 2


def lower_body(pos_ref, rr_ref, cr_ref, u_ref, fl_ref, fr_ref, top_ref, low_ref, o_ref, buf, sem):
    r, c = pos_ref[0], pos_ref[1]
    up = [ramp(r, rr_ref, ROWS, p) for p in (0, 1)]
    down = [ramp(r + 1, rr_ref, ROWS, p) for p in (-2, -1)]
    groups = (TC - 2) // GROUP

    def sends(g):
        at = pl.ds(g * 2 * GROUP, 2 * GROUP)
        return pltpu.make_async_copy(buf.at[:, at], o_ref.at[:, at], sem.at[g])

    def put(j, rows):
        v = jnp.swapaxes(rows, 0, 1)
        for b in range(2):
            buf[:, 2 * j + b] = v[VID * b : VID * (b + 1)]

    def rows_of(j, k):
        return u_ref[k, j]

    def inner(j):
        rows = []
        for p in range(16):
            v = rows_of(j, p)
            if p < 2:
                v = (v.astype(F32) * up[p] + top_ref[p, j + 1].astype(F32) * (1.0 - up[p])).astype(BF)
            elif p > 13:
                w = down[p - 14]
                v = (v.astype(F32) * (1.0 - w) + low_ref[p - 14, j + 1].astype(F32) * w).astype(BF)
            rows.append(v[None])
        put(j, jnp.concatenate(rows, axis=0))

    def outer(j, side_ref, slot, w):
        first = lax.broadcasted_iota(jnp.int32, (2 * VID, 1), 0) < VID
        w = jnp.where(first, w[0], w[1])

        def across(own, other):
            return own.astype(F32) * (1.0 - w) + other.astype(F32) * w

        rows = []
        for p in range(16):
            v = across(rows_of(j, p), side_ref[1 + p // 2, p % 2])
            if p < 2:
                v = v * up[p] + across(top_ref[p, j + 1], top_ref[p, slot]) * (1.0 - up[p])
            elif p > 13:
                k = down[p - 14]
                v = v * (1.0 - k) + across(low_ref[p - 14, j + 1], low_ref[p - 14, slot]) * k
            rows.append(v.astype(BF)[None])
        put(j, jnp.concatenate(rows, axis=0))

    outer(0, fl_ref, 0, [1.0 - ramp(c, cr_ref, COLS, x) for x in (0, 1)])
    for j in range(1, GROUP):
        inner(j)
    sends(0).start()

    def step(g, carry):
        for j in range(GROUP):
            inner(g * GROUP + j)
        sends(g).start()
        return carry

    lax.fori_loop(1, groups - 1, step, 0)
    for j in range(TC - 2 - GROUP, TC - 3):
        inner(j)
    outer(TC - 3, fr_ref, TC - 1, [ramp(c + 1, cr_ref, COLS, x) for x in (-2, -1)])
    sends(groups - 1).start()
    for g in range(groups):
        sends(g).wait()


def lower(pos, row_ramp, col_ramp, u, fl, fr, top, low):
    out = jax.ShapeDtypeStruct((VID, 2 * (TC - 2), 16, 2 * U), BF)
    return call(
        lower_body,
        "lower",
        out,
        (pos, row_ramp, col_ramp, u, fl, fr, top, low),
        1 << 20,
        scratch=[
            pltpu.VMEM((VID, 2 * (TC - 2), 16, 2 * U), BF),
            pltpu.SemaphoreType.DMA(((TC - 2) // GROUP,)),
        ],
        out_specs=pl.BlockSpec(memory_space=pltpu.HBM),
        smem=3,
    )


def per_device(
    latent_tokens,
    cache_latent,
    cache_middle,
    entry_weight,
    time_weight,
    up_weight,
    norm_gain,
    row_ramp,
    col_ramp,
):
    row_pos = lax.axis_index("rows")
    col_pos = lax.axis_index("cols")
    tok = jnp.transpose(latent_tokens, (0, 2, 1))
    before = shift(tok[:, :, 156:], "rows", 1)
    after = shift(tok[:, :, :52], "rows", -1)
    cache = jnp.transpose(cache_latent, (0, 1, 2, 4, 3))
    cm = jnp.transpose(cache_middle, (2, 3, 0, 1, 4)).reshape(TR * TC * VID, 2 * C)
    wt = time_weight.reshape(3 * C, 2 * C)
    ut = jnp.transpose(up_weight, (0, 1, 3, 2))
    gain = norm_gain.reshape(1, U)
    pos = jnp.stack([row_pos, col_pos]).astype(jnp.int32)
    w = fold(ut)
    x, we, dl, dr, left, right = edge(pos, tok, before, after, cache, entry_weight, cm, wt, w, gain)
    from_left = shift(right, "cols", 1)
    from_right = shift(left, "cols", -1)
    d = rest(x, we, cm, wt, dl, dr)
    top, low = join(*strips(d, w, gain), from_left, from_right)
    from_above = shift(low, "rows", 1)
    from_below = shift(top, "rows", -1)
    u = upper(d, w, gain, top)
    out = lower(pos, row_ramp, col_ramp, u, from_left, from_right, from_above, from_below)
    return jnp.transpose(out, (0, 2, 1, 3))


def solution(mesh):
    in_specs = (
        P(None, "rows", None),
        P(None, None, "rows", "cols", None),
        P(None, None, "rows", "cols", None),
        P(),
        P(),
        P(),
        P(),
        P(),
        P(),
    )
    out_specs = P(None, "rows", "cols", None)
    return jax.shard_map(
        per_device, mesh=mesh, in_specs=in_specs, out_specs=out_specs, check_vma=False
    )
```

```python
import functools

import jax
import jax.numpy as jnp
from jax import lax
from jax.experimental import pallas as pl
from jax.experimental.pallas import tpu as pltpu
from jax.sharding import PartitionSpec as P

EPSILON = 1e-06
BF = jnp.bfloat16
F32 = jnp.float32
VID, C, U = 8, 384, 192
TR, TC = 10, 28
ROWS, COLS = 32, 4
NT = (((1,), (1,)), ((), ()))


def shift(value, axis, step):
    size = lax.axis_size(axis)
    pairs = [(i, i + step) for i in range(size) if 0 <= i + step < size]
    return lax.ppermute(value, axis, pairs)


def swap(value, first):
    size = lax.axis_size("rows")
    pairs = [(i, i + 1) for i in range(first, size - 1, 2)]
    return lax.ppermute(value, "rows", pairs + [(j, i) for i, j in pairs])


VM = pl.BlockSpec(memory_space=pltpu.VMEM)
LIMIT = pltpu.CompilerParams(vmem_limit_bytes=24 << 20)


def held(value):
    return pltpu.with_memory_space_constraint(value, pltpu.VMEM)


def call(body, name, outs, args, flops, scratch=(), out_specs=None, smem=0):
    specs = [pl.BlockSpec(memory_space=pltpu.SMEM)] * smem + [VM] * (len(args) - smem)
    args = list(args[:smem]) + [held(v) for v in args[smem:]]
    return pl.pallas_call(
        body,
        in_specs=specs,
        out_specs=jax.tree.map(lambda _: VM, outs) if out_specs is None else out_specs,
        out_shape=outs,
        scratch_shapes=list(scratch),
        compiler_params=LIMIT,
        cost_estimate=pl.CostEstimate(flops=flops, bytes_accessed=1 << 16, transcendentals=0),
        name=name,
    )(*args)


WIDE = (TC + 2) * VID
PITCH = 56
STEPS = 5


def gather_body(col, tok_ref, before_ref, after_ref, cache_ref, x_ref, t_ref, lat_ref, old_ref):
    lat_ref[...] = jnp.zeros(lat_ref.shape, F32)
    old_ref[...] = jnp.zeros(old_ref.shape, F32)
    t_ref[...] = jnp.zeros(t_ref.shape, F32)
    for v in range(VID):
        own = jnp.transpose(tok_ref[v].astype(F32))
        rows = [jnp.transpose(before_ref[v].astype(F32))]
        rows += [own[52 * i : 52 * (i + 1)] for i in range(4)]
        rows += [jnp.transpose(after_ref[v].astype(F32))]
        for i in range(6):
            t_ref[v % 2, pl.ds(i * PITCH + 1, 52), 0:64] = rows[i]
        for i in range(6):
            near = t_ref[v % 2, pl.ds(i * PITCH + 13 * col, 15), :]
            for q in range(2):
                e = 2 * i + q
                if e in (0, 11):
                    continue
                for k in range(2):
                    part = pltpu.roll(near, (32 - (2 * q + k) * 16) % 128, 1)
                    part = part[1:15] if k == 0 else part[0:14]
                    first = 2 if k == 0 else 1
                    lat_ref[pl.ds((e * (TC + 2) + first) * VID + v, 14, stride=2 * VID), :] = part
        for t in range(TR):
            both = jnp.concatenate([cache_ref[v, 0, t], cache_ref[v, 1, t]], axis=0).astype(F32)
            both = jnp.concatenate([both, jnp.zeros((96, TC), F32)], axis=0)
            old_ref[pl.ds(((t + 1) * (TC + 2) + 1) * VID + v, TC, stride=VID), :] = jnp.transpose(both)
    lane = lax.broadcasted_iota(jnp.int32, (1, 128), 1)
    x_ref[...] = jnp.where(lane < 32, old_ref[...], jnp.where(lane < 48, lat_ref[...], 0.0)).astype(BF)


def mixed(x_ref, we_ref, cm_ref, wt_ref, areas):
    taps, olds, sizes = [], [], []
    for r0, nr, c0, nc in areas:
        for t in range(r0, r0 + nr):
            wide = (nc + 2) * VID
            at = [(t + k) * WIDE + c0 * VID for k in range(3)]
            taps.append(jnp.concatenate([x_ref[p : p + wide, 0:48] for p in at], axis=1))
            p = (t * TC + c0) * VID
            olds.append(cm_ref[p : p + nc * VID, :])
            sizes.append(nc)
    part = jnp.dot(jnp.concatenate(taps, axis=0), we_ref[...], preferred_element_type=F32)
    part = part.reshape(-1, VID, 3 * C)
    entry, at = [], 0
    for nc in sizes:
        three = [part[at + k : at + k + nc, :, k * C : (k + 1) * C] for k in range(3)]
        entry.append(three[0] + three[1] + three[2])
        at += nc + 2
    cells = sum(sizes)
    entry = jnp.concatenate(entry, axis=0).reshape(cells * VID, C).astype(BF)
    stacked = jnp.concatenate([jnp.concatenate(olds, axis=0), entry], axis=1)
    out = jnp.dot(stacked, wt_ref[...], preferred_element_type=F32).reshape(cells, 1, VID, 2 * C)
    out = jnp.concatenate([out[..., :C], out[..., C:]], axis=1)
    return out.reshape(cells, 2 * VID, C).astype(BF)


def edge_body(
    pos_ref,
    tok_ref,
    before_ref,
    after_ref,
    cache_ref,
    ew_ref,
    cm_ref,
    wt_ref,
    w_ref,
    gain_ref,
    x_ref,
    we_ref,
    dl_ref,
    dr_ref,
    left_ref,
    right_ref,
    t_ref,
    lat_ref,
    old_ref,
    sl_ref,
    sr_ref,
):
    dl_ref[...] = jnp.zeros(dl_ref.shape, BF)
    dr_ref[...] = jnp.zeros(dr_ref.shape, BF)
    for f in range(3):
        for kr in range(3):
            for kc in range(3):
                at = (kr * 3 + f) * 16
                we_ref[at : at + 16, kc * C : (kc + 1) * C] = ew_ref[f, kr, kc]
    gather_body(pos_ref[1], tok_ref, before_ref, after_ref, cache_ref, x_ref, t_ref, lat_ref, old_ref)
    d = mixed(x_ref, we_ref, cm_ref, wt_ref, ((0, TR, 0, 2), (0, TR, TC - 2, 2)))
    dl_ref[1 : TR + 1, 1:3] = d[: 2 * TR].reshape(TR, 2, 2 * VID, C)
    dr_ref[1 : TR + 1, 0:2] = d[2 * TR :].reshape(TR, 2, 2 * VID, C)
    sl_ref[...] = steps_right(dl_ref[...])
    sr_ref[...] = steps_right(dr_ref[...])
    gain = half_gain(gain_ref)
    for a in range(2):
        v = both(w_ref, gain, ((dl_ref, sl_ref, 0, TR, 0, 1), (dr_ref, sr_ref, 0, TR, 0, 1)), a)
        left_ref[:, a] = v[:TR]
        right_ref[:, a] = v[TR:]


def edge(pos, tok, before, after, cache, ew, cm, wt, w, gain):
    part = pltpu.VMEM((TR + 2, 3, 2 * VID, C), BF)
    side = jax.ShapeDtypeStruct((TR, 2, 2 * VID, 2 * U), BF)
    outs = (pltpu.VMEM((12 * WIDE, 128), BF), pltpu.VMEM((144, 3 * C), BF), part, part, side, side)
    return call(
        edge_body,
        "edge",
        outs,
        (pos, tok, before, after, cache, ew, cm, wt, w, gain),
        2 * 40000 * 65536,
        scratch=[
            pltpu.VMEM((2, 6 * PITCH + 8, 128), F32),
            pltpu.VMEM((12 * WIDE, 128), F32),
            pltpu.VMEM((12 * WIDE, 128), F32),
            pltpu.VMEM((TR + 2, 2, 2 * VID, C), BF),
            pltpu.VMEM((TR + 2, 2, 2 * VID, C), BF),
        ],
        smem=1,
    )


def rest_body(x_ref, we_ref, cm_ref, wt_ref, dl_ref, dr_ref, d_ref, s_ref):
    n = TC - 4
    line = jnp.zeros((1, n, 2 * VID, C), BF)
    d_ref[0:1, 3 : n + 3] = line
    d_ref[TR + 1 : TR + 2, 3 : n + 3] = line
    d_ref[:, 0:3] = dl_ref[...]
    d_ref[:, n + 3 : n + 6] = dr_ref[...]
    for i in (0, TR + 1):
        s_ref[i] = jnp.zeros((TC + 1, 2 * VID, C), BF)
    rows = TR // STEPS
    for g in range(STEPS):
        d = mixed(x_ref, we_ref, cm_ref, wt_ref, ((g * rows, rows, 2, n),))
        d_ref[1 + g * rows : 1 + (g + 1) * rows, 3 : n + 3] = d.reshape(rows, n, 2 * VID, C)
        for i in range(1 + g * rows, 1 + (g + 1) * rows):
            s_ref[i : i + 1] = steps_right(d_ref[i : i + 1])


def rest(x, we, cm, wt, dl, dr):
    outs = (pltpu.VMEM((TR + 2, TC + 2, 2 * VID, C), BF), pltpu.VMEM((TR + 2, TC + 1, 2 * VID, C), BF))
    return call(rest_body, "rest", outs, (x, we, cm, wt, dl, dr), 2 * 45000 * 65536)


def fold_body(ut_ref, w_ref):
    for a in range(2):
        for kr in range(2):
            rows = (((0,), (1, 2)), ((0, 1), (2,)))[a][kr]
            cols = [functools.reduce(jnp.add, [ut_ref[r, c].astype(F32) for r in rows]) for c in range(3)]
            for k, w in enumerate((cols[0] + cols[1] + cols[2], -cols[0], cols[2])):
                w = w.astype(BF)
                w_ref[a, k, 0:U, kr * C : (kr + 1) * C] = w
                w_ref[a, k, U:256, kr * C : (kr + 1) * C] = w[0:64]


def fold(ut):
    return call(fold_body, "fold", pltpu.VMEM((2, 3, 256, 2 * C), BF), (ut,), 1 << 24)


def steps_right(value):
    n = value.shape[1]
    return (value[:, 1:].astype(F32) - value[:, : n - 1].astype(F32)).astype(BF)


def activate(res, gain):
    cells = res.shape[0] // (2 * VID)
    res = res.reshape(cells, 2, VID, 256)
    one = res[:, 0].reshape(cells * VID, 256)
    two = res[:, 1].reshape(cells * VID, 256)
    low = lax.broadcasted_iota(jnp.int32, (1, 128), 1) < 64
    o0 = one[:, :128]
    o1 = jnp.where(low, one[:, 128:], two[:, 128:])
    o2 = jnp.where(low, two[:, 128:], two[:, :128])
    q1 = o1 * o1
    s0 = jnp.sum(o0 * o0 + jnp.where(low, q1, 0.0), axis=1, keepdims=True)
    s1 = jnp.sum(o2 * o2 + jnp.where(low, 0.0, q1), axis=1, keepdims=True)
    r0 = lax.rsqrt(s0 * (1.0 / U) + EPSILON)
    r1 = lax.rsqrt(s1 * (1.0 / U) + EPSILON)
    outs = []
    for k, (o, r) in enumerate(((o0, r0), (o1, jnp.where(low, r0, r1)), (o2, r1))):
        h = o * r * gain[:, 128 * k : 128 * (k + 1)]
        outs.append((h + h * jnp.tanh(h)).reshape(cells, 1, VID, 128))
    return outs


def both(w_ref, gain, areas, a):
    def pick(which, shift):
        parts = []
        for area in areas:
            ref, (i0, ni, j0, nj) = area[which], area[2:]
            taps = [
                ref[i0 + a + kr : i0 + a + kr + ni, j0 + shift : j0 + shift + nj].reshape(ni * nj * 2 * VID, C)
                for kr in range(2)
            ]
            parts.append(jnp.concatenate(taps, axis=1))
        return jnp.concatenate(parts, axis=0) if len(parts) > 1 else parts[0]

    def times(lhs, k):
        return lax.dot_general(lhs, w_ref[a, k], NT, preferred_element_type=F32)

    n = sum(area[3] * area[5] for area in areas)
    shared = times(pick(0, 1), 0)
    sides = [activate(shared + times(pick(1, b), 1 + b), gain) for b in range(2)]
    outs = [jnp.concatenate([u, v], axis=1).reshape(n, 2 * VID, 128).astype(BF) for u, v in zip(*sides)]
    outs[2] = jnp.concatenate([outs[2][:, :, 64:], outs[2][:, :, :64]], axis=2)
    return jnp.concatenate(outs, axis=2)


def half_gain(gain_ref):
    g = gain_ref[...] * 0.5
    return jnp.concatenate([g, g[:, :64], g[:, 128:], g[:, 64:128]], axis=1)


def strips_body(d_ref, s_ref, w_ref, gain_ref, top_ref, low_ref):
    gain = half_gain(gain_ref)
    n = TC - 2
    for a in range(2):
        for i, ref in ((0, top_ref), (TR - 1, low_ref)):
            ref[a] = both(w_ref, gain, ((d_ref, s_ref, i, 1, 1, n),), a)


def strips(d, s, w, gain):
    strip = pltpu.VMEM((2, TC - 2, 2 * VID, 2 * U), BF)
    return call(strips_body, "strips", (strip, strip), (d, s, w, gain), 2 * 832 * 18 * 65536)


def join_body(pos_ref, t_ref, l_ref, fl_ref, fr_ref, even_ref, odd_ref):
    n = TC - 2
    even = pos_ref[0] % 2 == 0

    def put(ref, own_ref, i):
        ref[:, 1 : n + 1] = own_ref[...]
        for a in range(2):
            ref[a, 0] = fl_ref[i, a]
            ref[a, n + 1] = fr_ref[i, a]

    @pl.when(even)
    def _():
        put(even_ref, l_ref, TR - 1)
        put(odd_ref, t_ref, 0)

    @pl.when(jnp.logical_not(even))
    def _():
        put(even_ref, t_ref, 0)
        put(odd_ref, l_ref, TR - 1)


def join(pos, t, l, fl, fr):
    strip = jax.ShapeDtypeStruct((2, TC, 2 * VID, 2 * U), BF)
    return call(join_body, "join", (strip, strip), (pos, t, l, fl, fr), 1 << 20, smem=1)


CHUNK = 26


def upper_body(d_ref, s_ref, w_ref, gain_ref, after_ref, o_ref):
    del after_ref
    gain = half_gain(gain_ref)
    for i in range(TR - 2):
        for a in range(2):
            for j in range(0, TC - 2, CHUNK):
                area = (d_ref, s_ref, i + 1, 1, 1 + j, CHUNK)
                o_ref[2 * i + a, j : j + CHUNK] = both(w_ref, gain, (area,), a)


def upper(d, s, w, gain, after):
    out = pltpu.VMEM((2 * (TR - 2), TC - 2, 2 * VID, 2 * U), BF)
    return call(upper_body, "upper", out, (d, s, w, gain, after), 2 * (TR - 2) * 416 * 18 * 65536)


def ramp(pos, table_ref, amount, place):
    step = table_ref[jnp.clip(pos, 1, amount - 1)].astype(F32)
    sloped = jnp.clip(jnp.full((1, 1), place + 0.5, F32) / jnp.full((1, 1), step, F32) + 0.5, 0.0, 1.0)
    return jnp.where(pos <= 0, 1.0, jnp.where(pos >= amount, 0.0, sloped))


GROUP = 2


def lower_body(pos_ref, rr_ref, cr_ref, u_ref, fl_ref, fr_ref, even_ref, odd_ref, o_ref, buf, sem):
    r, c = pos_ref[0], pos_ref[1]
    up = [ramp(r, rr_ref, ROWS, p) for p in (0, 1)]
    down = [ramp(r + 1, rr_ref, ROWS, p) for p in (-2, -1)]
    groups = (TC - 2) // GROUP
    even = jnp.full((2 * VID, 1), r % 2, jnp.int32) == 0

    def above(p, j):
        return jnp.where(even, odd_ref[p, j].astype(F32), even_ref[p, j].astype(F32))

    def below(p, j):
        return jnp.where(even, even_ref[p, j].astype(F32), odd_ref[p, j].astype(F32))

    def sends(g):
        at = pl.ds(g * 2 * GROUP, 2 * GROUP)
        return pltpu.make_async_copy(buf.at[:, at], o_ref.at[:, at], sem.at[g])

    def put(j, rows):
        v = jnp.swapaxes(rows, 0, 1)
        for b in range(2):
            buf[:, 2 * j + b] = v[VID * b : VID * (b + 1)]

    def rows_of(j, k):
        return u_ref[k, j]

    def inner(j):
        rows = []
        for p in range(16):
            v = rows_of(j, p)
            if p < 2:
                v = (v.astype(F32) * up[p] + above(p, j + 1) * (1.0 - up[p])).astype(BF)
            elif p > 13:
                w = down[p - 14]
                v = (v.astype(F32) * (1.0 - w) + below(p - 14, j + 1) * w).astype(BF)
            rows.append(v[None])
        put(j, jnp.concatenate(rows, axis=0))

    def outer(j, side_ref, slot, w):
        first = lax.broadcasted_iota(jnp.int32, (2 * VID, 1), 0) < VID
        w = jnp.where(first, w[0], w[1])

        def across(own, other):
            return own.astype(F32) * (1.0 - w) + other.astype(F32) * w

        rows = []
        for p in range(16):
            v = across(rows_of(j, p), side_ref[1 + p // 2, p % 2])
            if p < 2:
                v = v * up[p] + across(above(p, j + 1), above(p, slot)) * (1.0 - up[p])
            elif p > 13:
                k = down[p - 14]
                v = v * (1.0 - k) + across(below(p - 14, j + 1), below(p - 14, slot)) * k
            rows.append(v.astype(BF)[None])
        put(j, jnp.concatenate(rows, axis=0))

    outer(0, fl_ref, 0, [1.0 - ramp(c, cr_ref, COLS, x) for x in (0, 1)])
    for j in range(1, GROUP):
        inner(j)
    sends(0).start()

    def step(g, carry):
        for j in range(GROUP):
            inner(g * GROUP + j)
        sends(g).start()
        return carry

    lax.fori_loop(1, groups - 1, step, 0)
    for j in range(TC - 2 - GROUP, TC - 3):
        inner(j)
    outer(TC - 3, fr_ref, TC - 1, [ramp(c + 1, cr_ref, COLS, x) for x in (-2, -1)])
    sends(groups - 1).start()
    for g in range(groups):
        sends(g).wait()


def lower(pos, row_ramp, col_ramp, u, fl, fr, even, odd):
    out = jax.ShapeDtypeStruct((VID, 2 * (TC - 2), 16, 2 * U), BF)
    return call(
        lower_body,
        "lower",
        out,
        (pos, row_ramp, col_ramp, u, fl, fr, even, odd),
        1 << 20,
        scratch=[
            pltpu.VMEM((VID, 2 * (TC - 2), 16, 2 * U), BF),
            pltpu.SemaphoreType.DMA(((TC - 2) // GROUP,)),
        ],
        out_specs=pl.BlockSpec(memory_space=pltpu.HBM),
        smem=3,
    )


def per_device(
    latent_tokens,
    cache_latent,
    cache_middle,
    entry_weight,
    time_weight,
    up_weight,
    norm_gain,
    row_ramp,
    col_ramp,
):
    row_pos = lax.axis_index("rows")
    col_pos = lax.axis_index("cols")
    tok = jnp.transpose(latent_tokens, (0, 2, 1))
    before = shift(tok[:, :, 156:], "rows", 1)
    after = shift(tok[:, :, :52], "rows", -1)
    cache = jnp.transpose(cache_latent, (0, 1, 2, 4, 3))
    cm = jnp.transpose(cache_middle, (2, 3, 0, 1, 4)).reshape(TR * TC * VID, 2 * C)
    wt = time_weight.reshape(3 * C, 2 * C)
    ut = jnp.transpose(up_weight, (0, 1, 3, 2))
    gain = norm_gain.reshape(1, U)
    pos = jnp.stack([row_pos, col_pos]).astype(jnp.int32)
    w = fold(ut)
    x, we, dl, dr, left, right = edge(pos, tok, before, after, cache, entry_weight, cm, wt, w, gain)
    from_left = shift(right, "cols", 1)
    from_right = shift(left, "cols", -1)
    d, s = rest(x, we, cm, wt, dl, dr)
    to_even, to_odd = join(pos, *strips(d, s, w, gain), from_left, from_right)
    by_odd = swap(to_odd, 1)
    by_even = swap(to_even, 0)
    u = upper(d, s, w, gain, to_even)
    out = lower(pos, row_ramp, col_ramp, u, from_left, from_right, by_even, by_odd)
    return jnp.transpose(out, (0, 2, 1, 3))


def solution(mesh):
    in_specs = (
        P(None, "rows", None),
        P(None, None, "rows", "cols", None),
        P(None, None, "rows", "cols", None),
        P(),
        P(),
        P(),
        P(),
        P(),
        P(),
    )
    out_specs = P(None, "rows", "cols", None)
    return jax.shard_map(
        per_device, mesh=mesh, in_specs=in_specs, out_specs=out_specs, check_vma=False
    )
```

```python
import functools

import jax
import jax.numpy as jnp
from jax import lax
from jax.experimental import pallas as pl
from jax.experimental.pallas import tpu as pltpu
from jax.sharding import PartitionSpec as P

EPSILON = 1e-06
BF = jnp.bfloat16
F32 = jnp.float32
VID, C, U = 8, 384, 192
TR, TC = 10, 28
ROWS, COLS = 32, 4
NT = (((1,), (1,)), ((), ()))


def swap(value, axis, first):
    size = lax.axis_size(axis)
    pairs = [(i, i + 1) for i in range(first, size - 1, 2)]
    return lax.ppermute(value, axis, pairs + [(j, i) for i, j in pairs])


def either(pos, even, odd, rows):
    return jnp.where(jnp.full((rows, 1), pos % 2, jnp.int32) == 0, even, odd)


VM = pl.BlockSpec(memory_space=pltpu.VMEM)
LIMIT = pltpu.CompilerParams(vmem_limit_bytes=24 << 20)


def held(value):
    return pltpu.with_memory_space_constraint(value, pltpu.VMEM)


def call(body, name, outs, args, flops, scratch=(), out_specs=None, smem=0):
    specs = [pl.BlockSpec(memory_space=pltpu.SMEM)] * smem + [VM] * (len(args) - smem)
    args = list(args[:smem]) + [held(v) for v in args[smem:]]
    return pl.pallas_call(
        body,
        in_specs=specs,
        out_specs=jax.tree.map(lambda _: VM, outs) if out_specs is None else out_specs,
        out_shape=outs,
        scratch_shapes=list(scratch),
        compiler_params=LIMIT,
        cost_estimate=pl.CostEstimate(flops=flops, bytes_accessed=1 << 16, transcendentals=0),
        name=name,
    )(*args)


WIDE = (TC + 2) * VID
PITCH = 56
STEPS = 5


def gather_body(row, col, tok_ref, even_ref, odd_ref, cache_ref, x_ref, t_ref, lat_ref, old_ref):
    for ref in (lat_ref, old_ref):
        for e in (0, TR + 1):
            ref[e * WIDE : (e + 1) * WIDE, :] = jnp.zeros((WIDE, 128), F32)
        for e in range(1, TR + 1):
            for u in (0, TC + 1):
                at = e * WIDE + u * VID
                ref[at : at + VID, :] = jnp.zeros((VID, 128), F32)
    t_ref[...] = jnp.zeros(t_ref.shape, F32)
    for v in range(VID):
        own = jnp.transpose(tok_ref[v].astype(F32))
        by_even, by_odd = even_ref[v].astype(F32), odd_ref[v].astype(F32)
        rows = [jnp.transpose(either(row, by_odd, by_even, 64))]
        rows += [own[52 * i : 52 * (i + 1)] for i in range(4)]
        rows += [jnp.transpose(either(row, by_even, by_odd, 64))]
        for i in range(6):
            t_ref[v % 2, pl.ds(i * PITCH + 1, 52), 0:64] = rows[i]
        for i in range(6):
            near = t_ref[v % 2, pl.ds(i * PITCH + 13 * col, 15), :]
            for q in range(2):
                e = 2 * i + q
                if e in (0, 11):
                    continue
                for k in range(2):
                    part = pltpu.roll(near, (32 - (2 * q + k) * 16) % 128, 1)
                    part = part[1:15] if k == 0 else part[0:14]
                    first = 2 if k == 0 else 1
                    lat_ref[pl.ds((e * (TC + 2) + first) * VID + v, 14, stride=2 * VID), :] = part
        for t in range(TR):
            both = jnp.concatenate([cache_ref[v, 0, t], cache_ref[v, 1, t]], axis=0).astype(F32)
            both = jnp.concatenate([both, jnp.zeros((96, TC), F32)], axis=0)
            old_ref[pl.ds(((t + 1) * (TC + 2) + 1) * VID + v, TC, stride=VID), :] = jnp.transpose(both)
    lane = lax.broadcasted_iota(jnp.int32, (1, 128), 1)
    x_ref[...] = jnp.where(lane < 32, old_ref[...], jnp.where(lane < 48, lat_ref[...], 0.0)).astype(BF)


def mixed(x_ref, we_ref, cm_ref, wt_ref, areas):
    taps, olds, sizes = [], [], []
    for r0, nr, c0, nc in areas:
        for t in range(r0, r0 + nr):
            wide = (nc + 2) * VID
            at = [(t + k) * WIDE + c0 * VID for k in range(3)]
            taps.append(jnp.concatenate([x_ref[p : p + wide, 0:48] for p in at], axis=1))
            p = (t * TC + c0) * VID
            olds.append(cm_ref[p : p + nc * VID, :])
            sizes.append(nc)
    part = jnp.dot(jnp.concatenate(taps, axis=0), we_ref[...], preferred_element_type=F32)
    part = part.reshape(-1, VID, 3 * C)
    entry, at = [], 0
    for nc in sizes:
        three = [part[at + k : at + k + nc, :, k * C : (k + 1) * C] for k in range(3)]
        entry.append(three[0] + three[1] + three[2])
        at += nc + 2
    cells = sum(sizes)
    entry = jnp.concatenate(entry, axis=0).reshape(cells * VID, C).astype(BF)
    stacked = jnp.concatenate([jnp.concatenate(olds, axis=0), entry], axis=1)
    out = jnp.dot(stacked, wt_ref[...], preferred_element_type=F32).reshape(cells, 1, VID, 2 * C)
    out = jnp.concatenate([out[..., :C], out[..., C:]], axis=1)
    return out.reshape(cells, 2 * VID, C).astype(BF)


def edge_body(
    pos_ref,
    tok_ref,
    before_ref,
    after_ref,
    cache_ref,
    ew_ref,
    cm_ref,
    wt_ref,
    w_ref,
    gain_ref,
    x_ref,
    we_ref,
    dl_ref,
    dr_ref,
    even_ref,
    odd_ref,
    t_ref,
    lat_ref,
    old_ref,
    sl_ref,
    sr_ref,
):
    dl_ref[...] = jnp.zeros(dl_ref.shape, BF)
    dr_ref[...] = jnp.zeros(dr_ref.shape, BF)
    for f in range(3):
        for kr in range(3):
            for kc in range(3):
                at = (kr * 3 + f) * 16
                we_ref[at : at + 16, kc * C : (kc + 1) * C] = ew_ref[f, kr, kc]
    gather_body(pos_ref[0], pos_ref[1], tok_ref, before_ref, after_ref, cache_ref, x_ref, t_ref, lat_ref, old_ref)
    d = mixed(x_ref, we_ref, cm_ref, wt_ref, ((0, TR, 0, 2), (0, TR, TC - 2, 2)))
    dl_ref[1 : TR + 1, 1:3] = d[: 2 * TR].reshape(TR, 2, 2 * VID, C)
    dr_ref[1 : TR + 1, 0:2] = d[2 * TR :].reshape(TR, 2, 2 * VID, C)
    sl_ref[...] = steps_right(dl_ref[...])
    sr_ref[...] = steps_right(dr_ref[...])
    gain = half_gain(gain_ref)
    for a in range(2):
        v = both(w_ref, gain, ((dl_ref, sl_ref, 0, TR, 0, 1), (dr_ref, sr_ref, 0, TR, 0, 1)), a)
        even_ref[:, a] = either(pos_ref[1], v[TR:].astype(F32), v[:TR].astype(F32), 2 * VID).astype(BF)
        odd_ref[:, a] = either(pos_ref[1], v[:TR].astype(F32), v[TR:].astype(F32), 2 * VID).astype(BF)


def edge(pos, tok, before, after, cache, ew, cm, wt, w, gain):
    part = pltpu.VMEM((TR + 2, 3, 2 * VID, C), BF)
    side = jax.ShapeDtypeStruct((TR, 2, 2 * VID, 2 * U), BF)
    outs = (pltpu.VMEM((12 * WIDE, 128), BF), pltpu.VMEM((144, 3 * C), BF), part, part, side, side)
    return call(
        edge_body,
        "edge",
        outs,
        (pos, tok, before, after, cache, ew, cm, wt, w, gain),
        2 * 40000 * 65536,
        scratch=[
            pltpu.VMEM((2, 6 * PITCH + 8, 128), F32),
            pltpu.VMEM((12 * WIDE, 128), F32),
            pltpu.VMEM((12 * WIDE, 128), F32),
            pltpu.VMEM((TR + 2, 2, 2 * VID, C), BF),
            pltpu.VMEM((TR + 2, 2, 2 * VID, C), BF),
        ],
        smem=1,
    )


def rest_body(x_ref, we_ref, cm_ref, wt_ref, dl_ref, dr_ref, d_ref, s_ref):
    n = TC - 4
    line = jnp.zeros((1, n, 2 * VID, C), BF)
    d_ref[0:1, 3 : n + 3] = line
    d_ref[TR + 1 : TR + 2, 3 : n + 3] = line
    d_ref[:, 0:3] = dl_ref[...]
    d_ref[:, n + 3 : n + 6] = dr_ref[...]
    for i in (0, TR + 1):
        s_ref[i] = jnp.zeros((TC + 1, 2 * VID, C), BF)
    rows = TR // STEPS
    for g in range(STEPS):
        d = mixed(x_ref, we_ref, cm_ref, wt_ref, ((g * rows, rows, 2, n),))
        d_ref[1 + g * rows : 1 + (g + 1) * rows, 3 : n + 3] = d.reshape(rows, n, 2 * VID, C)
        for i in range(1 + g * rows, 1 + (g + 1) * rows):
            s_ref[i : i + 1] = steps_right(d_ref[i : i + 1])


def rest(x, we, cm, wt, dl, dr):
    outs = (pltpu.VMEM((TR + 2, TC + 2, 2 * VID, C), BF), pltpu.VMEM((TR + 2, TC + 1, 2 * VID, C), BF))
    return call(rest_body, "rest", outs, (x, we, cm, wt, dl, dr), 2 * 45000 * 65536)


def fold_body(ut_ref, w_ref):
    for a in range(2):
        for kr in range(2):
            rows = (((0,), (1, 2)), ((0, 1), (2,)))[a][kr]
            cols = [functools.reduce(jnp.add, [ut_ref[r, c].astype(F32) for r in rows]) for c in range(3)]
            for k, w in enumerate((cols[0] + cols[1] + cols[2], -cols[0], cols[2])):
                w = w.astype(BF)
                w_ref[a, k, 0:U, kr * C : (kr + 1) * C] = w
                w_ref[a, k, U:256, kr * C : (kr + 1) * C] = w[0:64]


def fold(ut):
    return call(fold_body, "fold", pltpu.VMEM((2, 3, 256, 2 * C), BF), (ut,), 1 << 24)


def steps_right(value):
    n = value.shape[1]
    return (value[:, 1:].astype(F32) - value[:, : n - 1].astype(F32)).astype(BF)


def activate(res, gain):
    cells = res.shape[0] // (2 * VID)
    res = res.reshape(cells, 2, VID, 256)
    one = res[:, 0].reshape(cells * VID, 256)
    two = res[:, 1].reshape(cells * VID, 256)
    low = lax.broadcasted_iota(jnp.int32, (1, 128), 1) < 64
    o0 = one[:, :128]
    o1 = jnp.where(low, one[:, 128:], two[:, 128:])
    o2 = jnp.where(low, two[:, 128:], two[:, :128])
    q1 = o1 * o1
    s0 = jnp.sum(o0 * o0 + jnp.where(low, q1, 0.0), axis=1, keepdims=True)
    s1 = jnp.sum(o2 * o2 + jnp.where(low, 0.0, q1), axis=1, keepdims=True)
    r0 = lax.rsqrt(s0 * (1.0 / U) + EPSILON)
    r1 = lax.rsqrt(s1 * (1.0 / U) + EPSILON)
    outs = []
    for k, (o, r) in enumerate(((o0, r0), (o1, jnp.where(low, r0, r1)), (o2, r1))):
        h = o * r * gain[:, 128 * k : 128 * (k + 1)]
        outs.append((h + h * jnp.tanh(h)).reshape(cells, 1, VID, 128))
    return outs


def both(w_ref, gain, areas, a):
    def pick(which, shift):
        parts = []
        for area in areas:
            ref, (i0, ni, j0, nj) = area[which], area[2:]
            taps = [
                ref[i0 + a + kr : i0 + a + kr + ni, j0 + shift : j0 + shift + nj].reshape(ni * nj * 2 * VID, C)
                for kr in range(2)
            ]
            parts.append(jnp.concatenate(taps, axis=1))
        return jnp.concatenate(parts, axis=0) if len(parts) > 1 else parts[0]

    def times(lhs, k):
        return lax.dot_general(lhs, w_ref[a, k], NT, preferred_element_type=F32)

    n = sum(area[3] * area[5] for area in areas)
    shared = times(pick(0, 1), 0)
    sides = [activate(shared + times(pick(1, b), 1 + b), gain) for b in range(2)]
    outs = [jnp.concatenate([u, v], axis=1).reshape(n, 2 * VID, 128).astype(BF) for u, v in zip(*sides)]
    outs[2] = jnp.concatenate([outs[2][:, :, 64:], outs[2][:, :, :64]], axis=2)
    return jnp.concatenate(outs, axis=2)


def half_gain(gain_ref):
    g = gain_ref[...] * 0.5
    return jnp.concatenate([g, g[:, :64], g[:, 128:], g[:, 64:128]], axis=1)


def strips_body(d_ref, s_ref, w_ref, gain_ref, top_ref, low_ref):
    gain = half_gain(gain_ref)
    n = TC - 2
    for a in range(2):
        for i, ref in ((0, top_ref), (TR - 1, low_ref)):
            ref[a] = both(w_ref, gain, ((d_ref, s_ref, i, 1, 1, n),), a)


def strips(d, s, w, gain):
    strip = pltpu.VMEM((2, TC - 2, 2 * VID, 2 * U), BF)
    return call(strips_body, "strips", (strip, strip), (d, s, w, gain), 2 * 832 * 18 * 65536)


def join_body(pos_ref, t_ref, l_ref, se_ref, so_ref, even_ref, odd_ref):
    n = TC - 2
    even = pos_ref[0] % 2 == 0

    def put(ref, own_ref, i):
        ref[:, 1 : n + 1] = own_ref[...]
        for a in range(2):
            by_even, by_odd = se_ref[i, a].astype(F32), so_ref[i, a].astype(F32)
            ref[a, 0] = either(pos_ref[1], by_odd, by_even, 2 * VID).astype(BF)
            ref[a, n + 1] = either(pos_ref[1], by_even, by_odd, 2 * VID).astype(BF)

    @pl.when(even)
    def _():
        put(even_ref, l_ref, TR - 1)
        put(odd_ref, t_ref, 0)

    @pl.when(jnp.logical_not(even))
    def _():
        put(even_ref, t_ref, 0)
        put(odd_ref, l_ref, TR - 1)


def join(pos, t, l, fl, fr):
    strip = jax.ShapeDtypeStruct((2, TC, 2 * VID, 2 * U), BF)
    return call(join_body, "join", (strip, strip), (pos, t, l, fl, fr), 1 << 20, smem=1)


CHUNK = 26


def upper_body(d_ref, s_ref, w_ref, gain_ref, after_ref, o_ref):
    del after_ref
    gain = half_gain(gain_ref)
    for i in range(TR - 2):
        for a in range(2):
            for j in range(0, TC - 2, CHUNK):
                area = (d_ref, s_ref, i + 1, 1, 1 + j, CHUNK)
                o_ref[2 * i + a, j : j + CHUNK] = both(w_ref, gain, (area,), a)


def upper(d, s, w, gain, after):
    out = pltpu.VMEM((2 * (TR - 2), TC - 2, 2 * VID, 2 * U), BF)
    return call(upper_body, "upper", out, (d, s, w, gain, after), 2 * (TR - 2) * 416 * 18 * 65536)


def ramp(pos, table_ref, amount, place):
    step = table_ref[jnp.clip(pos, 1, amount - 1)].astype(F32)
    sloped = jnp.clip(jnp.full((1, 1), place + 0.5, F32) / jnp.full((1, 1), step, F32) + 0.5, 0.0, 1.0)
    return jnp.where(pos <= 0, 1.0, jnp.where(pos >= amount, 0.0, sloped))


GROUP = 2


def lower_body(pos_ref, rr_ref, cr_ref, u_ref, se_ref, so_ref, even_ref, odd_ref, o_ref, buf, sem):
    r, c = pos_ref[0], pos_ref[1]
    up = [ramp(r, rr_ref, ROWS, p) for p in (0, 1)]
    down = [ramp(r + 1, rr_ref, ROWS, p) for p in (-2, -1)]
    groups = (TC - 2) // GROUP

    def above(p, j):
        return either(r, odd_ref[p, j].astype(F32), even_ref[p, j].astype(F32), 2 * VID)

    def below(p, j):
        return either(r, even_ref[p, j].astype(F32), odd_ref[p, j].astype(F32), 2 * VID)

    def left(i, a):
        return either(c, so_ref[i, a].astype(F32), se_ref[i, a].astype(F32), 2 * VID)

    def right(i, a):
        return either(c, se_ref[i, a].astype(F32), so_ref[i, a].astype(F32), 2 * VID)

    def sends(g):
        at = pl.ds(g * 2 * GROUP, 2 * GROUP)
        return pltpu.make_async_copy(buf.at[:, at], o_ref.at[:, at], sem.at[g])

    def put(j, rows):
        v = jnp.swapaxes(rows, 0, 1)
        for b in range(2):
            buf[:, 2 * j + b] = v[VID * b : VID * (b + 1)]

    def rows_of(j, k):
        return u_ref[k, j]

    def inner(j):
        rows = []
        for p in range(16):
            v = rows_of(j, p)
            if p < 2:
                v = (v.astype(F32) * up[p] + above(p, j + 1) * (1.0 - up[p])).astype(BF)
            elif p > 13:
                w = down[p - 14]
                v = (v.astype(F32) * (1.0 - w) + below(p - 14, j + 1) * w).astype(BF)
            rows.append(v[None])
        put(j, jnp.concatenate(rows, axis=0))

    def outer(j, side, slot, w):
        first = lax.broadcasted_iota(jnp.int32, (2 * VID, 1), 0) < VID
        w = jnp.where(first, w[0], w[1])

        def across(own, other):
            return own.astype(F32) * (1.0 - w) + other.astype(F32) * w

        rows = []
        for p in range(16):
            v = across(rows_of(j, p), side(1 + p // 2, p % 2))
            if p < 2:
                v = v * up[p] + across(above(p, j + 1), above(p, slot)) * (1.0 - up[p])
            elif p > 13:
                k = down[p - 14]
                v = v * (1.0 - k) + across(below(p - 14, j + 1), below(p - 14, slot)) * k
            rows.append(v.astype(BF)[None])
        put(j, jnp.concatenate(rows, axis=0))

    outer(0, left, 0, [1.0 - ramp(c, cr_ref, COLS, x) for x in (0, 1)])
    for j in range(1, GROUP):
        inner(j)
    sends(0).start()

    def step(g, carry):
        for j in range(GROUP):
            inner(g * GROUP + j)
        sends(g).start()
        return carry

    lax.fori_loop(1, groups - 1, step, 0)
    for j in range(TC - 2 - GROUP, TC - 3):
        inner(j)
    outer(TC - 3, right, TC - 1, [ramp(c + 1, cr_ref, COLS, x) for x in (-2, -1)])
    sends(groups - 1).start()
    for g in range(groups):
        sends(g).wait()


def lower(pos, row_ramp, col_ramp, u, fl, fr, even, odd):
    out = jax.ShapeDtypeStruct((VID, 2 * (TC - 2), 16, 2 * U), BF)
    return call(
        lower_body,
        "lower",
        out,
        (pos, row_ramp, col_ramp, u, fl, fr, even, odd),
        1 << 20,
        scratch=[
            pltpu.VMEM((VID, 2 * (TC - 2), 16, 2 * U), BF),
            pltpu.SemaphoreType.DMA(((TC - 2) // GROUP,)),
        ],
        out_specs=pl.BlockSpec(memory_space=pltpu.HBM),
        smem=3,
    )


def per_device(
    latent_tokens,
    cache_latent,
    cache_middle,
    entry_weight,
    time_weight,
    up_weight,
    norm_gain,
    row_ramp,
    col_ramp,
):
    row_pos = lax.axis_index("rows")
    col_pos = lax.axis_index("cols")
    tok = jnp.transpose(latent_tokens, (0, 2, 1))
    first, last = tok[:, :, :52], tok[:, :, 156:]
    even = row_pos % 2 == 0
    by_odd = swap(jnp.where(even, first, last), "rows", 1)
    by_even = swap(jnp.where(even, last, first), "rows", 0)
    cache = jnp.transpose(cache_latent, (0, 1, 2, 4, 3))
    cm = jnp.transpose(cache_middle, (2, 3, 0, 1, 4)).reshape(TR * TC * VID, 2 * C)
    wt = time_weight.reshape(3 * C, 2 * C)
    ut = jnp.transpose(up_weight, (0, 1, 3, 2))
    gain = norm_gain.reshape(1, U)
    pos = jnp.stack([row_pos, col_pos]).astype(jnp.int32)
    w = fold(ut)
    x, we, dl, dr, side_even, side_odd = edge(pos, tok, by_even, by_odd, cache, entry_weight, cm, wt, w, gain)
    side_even = swap(side_even, "cols", 0)
    side_odd = swap(side_odd, "cols", 1)
    d, s = rest(x, we, cm, wt, dl, dr)
    to_even, to_odd = join(pos, *strips(d, s, w, gain), side_even, side_odd)
    by_odd = swap(to_odd, "rows", 1)
    by_even = swap(to_even, "rows", 0)
    u = upper(d, s, w, gain, to_even)
    out = lower(pos, row_ramp, col_ramp, u, side_even, side_odd, by_even, by_odd)
    return jnp.transpose(out, (0, 2, 1, 3))


def solution(mesh):
    in_specs = (
        P(None, "rows", None),
        P(None, None, "rows", "cols", None),
        P(None, None, "rows", "cols", None),
        P(),
        P(),
        P(),
        P(),
        P(),
        P(),
    )
    out_specs = P(None, "rows", "cols", None)
    return jax.shard_map(
        per_device, mesh=mesh, in_specs=in_specs, out_specs=out_specs, check_vma=False
    )
```

```python
import functools

import jax
import jax.numpy as jnp
from jax import lax
from jax.experimental import pallas as pl
from jax.experimental.pallas import tpu as pltpu
from jax.sharding import PartitionSpec as P

EPSILON = 1e-06
BF = jnp.bfloat16
F32 = jnp.float32
VID, C, U = 8, 384, 192
TR, TC = 10, 28
ROWS, COLS = 32, 4
NT = (((1,), (1,)), ((), ()))


def swap(value, axis, first):
    size = lax.axis_size(axis)
    pairs = [(i, i + 1) for i in range(first, size - 1, 2)]
    return lax.ppermute(value, axis, pairs + [(j, i) for i, j in pairs])


def either(pos, even, odd, rows):
    return jnp.where(jnp.full((rows, 1), pos % 2, jnp.int32) == 0, even, odd)


VM = pl.BlockSpec(memory_space=pltpu.VMEM)
LIMIT = pltpu.CompilerParams(vmem_limit_bytes=24 << 20)


def held(value):
    return pltpu.with_memory_space_constraint(value, pltpu.VMEM)


def call(body, name, outs, args, flops, scratch=(), out_specs=None, smem=0):
    specs = [pl.BlockSpec(memory_space=pltpu.SMEM)] * smem + [VM] * (len(args) - smem)
    args = list(args[:smem]) + [held(v) for v in args[smem:]]
    return pl.pallas_call(
        body,
        in_specs=specs,
        out_specs=jax.tree.map(lambda _: VM, outs) if out_specs is None else out_specs,
        out_shape=outs,
        scratch_shapes=list(scratch),
        compiler_params=LIMIT,
        cost_estimate=pl.CostEstimate(flops=flops, bytes_accessed=1 << 16, transcendentals=0),
        name=name,
    )(*args)


WIDE = (TC + 2) * VID
PITCH = 56


def gather_body(row, col, tok_ref, even_ref, odd_ref, cache_ref, x_ref, t_ref, lat_ref, old_ref):
    for ref in (lat_ref, old_ref):
        for e in (0, TR + 1):
            ref[e * WIDE : (e + 1) * WIDE, :] = jnp.zeros((WIDE, 128), F32)
        for e in range(1, TR + 1):
            for u in (0, TC + 1):
                at = e * WIDE + u * VID
                ref[at : at + VID, :] = jnp.zeros((VID, 128), F32)
    t_ref[...] = jnp.zeros(t_ref.shape, F32)
    for v in range(VID):
        own = jnp.transpose(tok_ref[v].astype(F32))
        by_even, by_odd = even_ref[v].astype(F32), odd_ref[v].astype(F32)
        rows = [jnp.transpose(either(row, by_odd, by_even, 64))]
        rows += [own[52 * i : 52 * (i + 1)] for i in range(4)]
        rows += [jnp.transpose(either(row, by_even, by_odd, 64))]
        for i in range(6):
            t_ref[v % 2, pl.ds(i * PITCH + 1, 52), 0:64] = rows[i]
        for i in range(6):
            near = t_ref[v % 2, pl.ds(i * PITCH + 13 * col, 15), :]
            for q in range(2):
                e = 2 * i + q
                if e in (0, 11):
                    continue
                for k in range(2):
                    part = pltpu.roll(near, (32 - (2 * q + k) * 16) % 128, 1)
                    part = part[1:15] if k == 0 else part[0:14]
                    first = 2 if k == 0 else 1
                    lat_ref[pl.ds((e * (TC + 2) + first) * VID + v, 14, stride=2 * VID), :] = part
        for t in range(TR):
            both = jnp.concatenate([cache_ref[v, 0, t], cache_ref[v, 1, t]], axis=0).astype(F32)
            both = jnp.concatenate([both, jnp.zeros((96, TC), F32)], axis=0)
            old_ref[pl.ds(((t + 1) * (TC + 2) + 1) * VID + v, TC, stride=VID), :] = jnp.transpose(both)
    lane = lax.broadcasted_iota(jnp.int32, (1, 128), 1)
    x_ref[...] = jnp.where(lane < 32, old_ref[...], jnp.where(lane < 48, lat_ref[...], 0.0)).astype(BF)


def mixed(x_ref, we_ref, cm_ref, wt_ref, areas):
    taps, olds, sizes = [], [], []
    for r0, nr, c0, nc in areas:
        for t in range(r0, r0 + nr):
            wide = (nc + 2) * VID
            at = [(t + k) * WIDE + c0 * VID for k in range(3)]
            taps.append(jnp.concatenate([x_ref[p : p + wide, 0:48] for p in at], axis=1))
            p = (t * TC + c0) * VID
            olds.append(cm_ref[p : p + nc * VID, :])
            sizes.append(nc)
    part = jnp.dot(jnp.concatenate(taps, axis=0), we_ref[...], preferred_element_type=F32)
    part = part.reshape(-1, VID, 3 * C)
    entry, at = [], 0
    for nc in sizes:
        three = [part[at + k : at + k + nc, :, k * C : (k + 1) * C] for k in range(3)]
        entry.append(three[0] + three[1] + three[2])
        at += nc + 2
    cells = sum(sizes)
    entry = jnp.concatenate(entry, axis=0).reshape(cells * VID, C).astype(BF)
    stacked = jnp.concatenate([jnp.concatenate(olds, axis=0), entry], axis=1)
    out = jnp.dot(stacked, wt_ref[...], preferred_element_type=F32).reshape(cells, 1, VID, 2 * C)
    out = jnp.concatenate([out[..., :C], out[..., C:]], axis=1)
    return out.reshape(cells, 2 * VID, C).astype(BF)


def edge_body(
    pos_ref,
    tok_ref,
    before_ref,
    after_ref,
    cache_ref,
    ew_ref,
    cm_ref,
    wt_ref,
    w_ref,
    gain_ref,
    x_ref,
    we_ref,
    dl_ref,
    dr_ref,
    even_ref,
    odd_ref,
    t_ref,
    lat_ref,
    old_ref,
    sl_ref,
    sr_ref,
):
    dl_ref[...] = jnp.zeros(dl_ref.shape, BF)
    dr_ref[...] = jnp.zeros(dr_ref.shape, BF)
    for f in range(3):
        for kr in range(3):
            for kc in range(3):
                at = (kr * 3 + f) * 16
                we_ref[at : at + 16, kc * C : (kc + 1) * C] = ew_ref[f, kr, kc]
    gather_body(pos_ref[0], pos_ref[1], tok_ref, before_ref, after_ref, cache_ref, x_ref, t_ref, lat_ref, old_ref)
    d = mixed(x_ref, we_ref, cm_ref, wt_ref, ((0, TR, 0, 2), (0, TR, TC - 2, 2)))
    dl_ref[1 : TR + 1, 1:3] = d[: 2 * TR].reshape(TR, 2, 2 * VID, C)
    dr_ref[1 : TR + 1, 0:2] = d[2 * TR :].reshape(TR, 2, 2 * VID, C)
    sl_ref[...] = steps_right(dl_ref[...])
    sr_ref[...] = steps_right(dr_ref[...])
    gain = half_gain(gain_ref)
    for a in range(2):
        v = both(w_ref, gain, ((dl_ref, sl_ref, 0, TR, 0, 1), (dr_ref, sr_ref, 0, TR, 0, 1)), a)
        even_ref[:, a] = either(pos_ref[1], v[TR:].astype(F32), v[:TR].astype(F32), 2 * VID).astype(BF)
        odd_ref[:, a] = either(pos_ref[1], v[:TR].astype(F32), v[TR:].astype(F32), 2 * VID).astype(BF)


def edge(pos, tok, before, after, cache, ew, cm, wt, w, gain):
    part = pltpu.VMEM((TR + 2, 3, 2 * VID, C), BF)
    side = jax.ShapeDtypeStruct((TR, 2, 2 * VID, 2 * U), BF)
    outs = (pltpu.VMEM((12 * WIDE, 128), BF), pltpu.VMEM((144, 3 * C), BF), part, part, side, side)
    return call(
        edge_body,
        "edge",
        outs,
        (pos, tok, before, after, cache, ew, cm, wt, w, gain),
        2 * 40000 * 65536,
        scratch=[
            pltpu.VMEM((2, 6 * PITCH + 8, 128), F32),
            pltpu.VMEM((12 * WIDE, 128), F32),
            pltpu.VMEM((12 * WIDE, 128), F32),
            pltpu.VMEM((TR + 2, 2, 2 * VID, C), BF),
            pltpu.VMEM((TR + 2, 2, 2 * VID, C), BF),
        ],
        smem=1,
    )


def ends_body(x_ref, we_ref, cm_ref, wt_ref, dl_ref, dr_ref, td_ref, ts_ref, ld_ref, ls_ref):
    n = TC - 4
    for d_ref, s_ref, first, line, row in ((td_ref, ts_ref, 0, 0, 0), (ld_ref, ls_ref, TR - 1, 2, TR - 2)):
        d_ref[line, 3 : n + 3] = jnp.zeros((n, 2 * VID, C), BF)
        d_ref[:, 0:3] = dl_ref[first : first + 3]
        d_ref[:, n + 3 : n + 6] = dr_ref[first : first + 3]
        d = mixed(x_ref, we_ref, cm_ref, wt_ref, ((row, 2, 2, n),))
        at = 1 if line == 0 else 0
        d_ref[at : at + 2, 3 : n + 3] = d.reshape(2, n, 2 * VID, C)
        for i in range(3):
            s_ref[i : i + 1] = steps_right(d_ref[i : i + 1])


def ends(x, we, cm, wt, dl, dr):
    part = pltpu.VMEM((3, TC + 2, 2 * VID, C), BF)
    step = pltpu.VMEM((3, TC + 1, 2 * VID, C), BF)
    return call(ends_body, "ends", (part, step, part, step), (x, we, cm, wt, dl, dr), 2 * 18000 * 65536)


def rest_body(x_ref, we_ref, cm_ref, wt_ref, dl_ref, dr_ref, td_ref, ts_ref, ld_ref, ls_ref, d_ref, s_ref):
    n = TC - 4
    d_ref[0:3] = td_ref[...]
    s_ref[0:3] = ts_ref[...]
    d_ref[TR - 1 : TR + 2] = ld_ref[...]
    s_ref[TR - 1 : TR + 2] = ls_ref[...]
    d_ref[3 : TR - 1, 0:3] = dl_ref[3 : TR - 1]
    d_ref[3 : TR - 1, n + 3 : n + 6] = dr_ref[3 : TR - 1]
    for row in range(2, TR - 2, 2):
        d = mixed(x_ref, we_ref, cm_ref, wt_ref, ((row, 2, 2, n),))
        d_ref[1 + row : 3 + row, 3 : n + 3] = d.reshape(2, n, 2 * VID, C)
        for i in range(1 + row, 3 + row):
            s_ref[i : i + 1] = steps_right(d_ref[i : i + 1])


def fold_body(ut_ref, w_ref):
    for a in range(2):
        for kr in range(2):
            rows = (((0,), (1, 2)), ((0, 1), (2,)))[a][kr]
            cols = [functools.reduce(jnp.add, [ut_ref[r, c].astype(F32) for r in rows]) for c in range(3)]
            for k, w in enumerate((cols[0] + cols[1] + cols[2], -cols[0], cols[2])):
                w = w.astype(BF)
                w_ref[a, k, 0:U, kr * C : (kr + 1) * C] = w
                w_ref[a, k, U:256, kr * C : (kr + 1) * C] = w[0:64]


def fold(ut):
    return call(fold_body, "fold", pltpu.VMEM((2, 3, 256, 2 * C), BF), (ut,), 1 << 24)


def steps_right(value):
    n = value.shape[1]
    return (value[:, 1:].astype(F32) - value[:, : n - 1].astype(F32)).astype(BF)


def activate(res, gain):
    cells = res.shape[0] // (2 * VID)
    res = res.reshape(cells, 2, VID, 256)
    one = res[:, 0].reshape(cells * VID, 256)
    two = res[:, 1].reshape(cells * VID, 256)
    low = lax.broadcasted_iota(jnp.int32, (1, 128), 1) < 64
    o0 = one[:, :128]
    o1 = jnp.where(low, one[:, 128:], two[:, 128:])
    o2 = jnp.where(low, two[:, 128:], two[:, :128])
    q1 = o1 * o1
    s0 = jnp.sum(o0 * o0 + jnp.where(low, q1, 0.0), axis=1, keepdims=True)
    s1 = jnp.sum(o2 * o2 + jnp.where(low, 0.0, q1), axis=1, keepdims=True)
    r0 = lax.rsqrt(s0 * (1.0 / U) + EPSILON)
    r1 = lax.rsqrt(s1 * (1.0 / U) + EPSILON)
    outs = []
    for k, (o, r) in enumerate(((o0, r0), (o1, jnp.where(low, r0, r1)), (o2, r1))):
        h = o * r * gain[:, 128 * k : 128 * (k + 1)]
        outs.append((h + h * jnp.tanh(h)).reshape(cells, 1, VID, 128))
    return outs


def both(w_ref, gain, areas, a):
    def pick(which, shift):
        parts = []
        for area in areas:
            ref, (i0, ni, j0, nj) = area[which], area[2:]
            taps = [
                ref[i0 + a + kr : i0 + a + kr + ni, j0 + shift : j0 + shift + nj].reshape(ni * nj * 2 * VID, C)
                for kr in range(2)
            ]
            parts.append(jnp.concatenate(taps, axis=1))
        return jnp.concatenate(parts, axis=0) if len(parts) > 1 else parts[0]

    def times(lhs, k):
        return lax.dot_general(lhs, w_ref[a, k], NT, preferred_element_type=F32)

    n = sum(area[3] * area[5] for area in areas)
    shared = times(pick(0, 1), 0)
    sides = [activate(shared + times(pick(1, b), 1 + b), gain) for b in range(2)]
    outs = [jnp.concatenate([u, v], axis=1).reshape(n, 2 * VID, 128).astype(BF) for u, v in zip(*sides)]
    outs[2] = jnp.concatenate([outs[2][:, :, 64:], outs[2][:, :, :64]], axis=2)
    return jnp.concatenate(outs, axis=2)


def half_gain(gain_ref):
    g = gain_ref[...] * 0.5
    return jnp.concatenate([g, g[:, :64], g[:, 128:], g[:, 64:128]], axis=1)


def strips_body(td_ref, ts_ref, ld_ref, ls_ref, w_ref, gain_ref, top_ref, low_ref):
    gain = half_gain(gain_ref)
    n = TC - 2
    for a in range(2):
        for d_ref, s_ref, ref in ((td_ref, ts_ref, top_ref), (ld_ref, ls_ref, low_ref)):
            ref[a] = both(w_ref, gain, ((d_ref, s_ref, 0, 1, 1, n),), a)


def strips(rows, w, gain):
    strip = pltpu.VMEM((2, TC - 2, 2 * VID, 2 * U), BF)
    return call(strips_body, "strips", (strip, strip), (*rows, w, gain), 2 * 832 * 18 * 65536)


def join_body(pos_ref, t_ref, l_ref, se_ref, so_ref, even_ref, odd_ref):
    n = TC - 2
    even = pos_ref[0] % 2 == 0

    def put(ref, own_ref, i):
        ref[:, 1 : n + 1] = own_ref[...]
        for a in range(2):
            by_even, by_odd = se_ref[i, a].astype(F32), so_ref[i, a].astype(F32)
            ref[a, 0] = either(pos_ref[1], by_odd, by_even, 2 * VID).astype(BF)
            ref[a, n + 1] = either(pos_ref[1], by_even, by_odd, 2 * VID).astype(BF)

    @pl.when(even)
    def _():
        put(even_ref, l_ref, TR - 1)
        put(odd_ref, t_ref, 0)

    @pl.when(jnp.logical_not(even))
    def _():
        put(even_ref, t_ref, 0)
        put(odd_ref, l_ref, TR - 1)


def join(pos, t, l, fl, fr):
    strip = jax.ShapeDtypeStruct((2, TC, 2 * VID, 2 * U), BF)
    return call(join_body, "join", (strip, strip), (pos, t, l, fl, fr), 1 << 20, smem=1)


def upper_body(*refs):
    parts, (w_ref, gain_ref, _, o_ref, d_ref, s_ref) = refs[:10], refs[10:]
    rest_body(*parts, d_ref, s_ref)
    gain = half_gain(gain_ref)
    for i in range(TR - 2):
        for a in range(2):
            o_ref[2 * i + a] = both(w_ref, gain, ((d_ref, s_ref, i + 1, 1, 1, TC - 2),), a)


def upper(parts, w, gain, after):
    return call(
        upper_body,
        "upper",
        pltpu.VMEM((2 * (TR - 2), TC - 2, 2 * VID, 2 * U), BF),
        (*parts, w, gain, after),
        2 * (27000 + (TR - 2) * 416 * 18) * 65536,
        scratch=[
            pltpu.VMEM((TR + 2, TC + 2, 2 * VID, C), BF),
            pltpu.VMEM((TR + 2, TC + 1, 2 * VID, C), BF),
        ],
    )


def ramp(pos, table_ref, amount, place):
    step = table_ref[jnp.clip(pos, 1, amount - 1)].astype(F32)
    sloped = jnp.clip(jnp.full((1, 1), place + 0.5, F32) / jnp.full((1, 1), step, F32) + 0.5, 0.0, 1.0)
    return jnp.where(pos <= 0, 1.0, jnp.where(pos >= amount, 0.0, sloped))


GROUP = 2


def lower_body(pos_ref, rr_ref, cr_ref, u_ref, se_ref, so_ref, even_ref, odd_ref, o_ref, buf, sem):
    r, c = pos_ref[0], pos_ref[1]
    up = [ramp(r, rr_ref, ROWS, p) for p in (0, 1)]
    down = [ramp(r + 1, rr_ref, ROWS, p) for p in (-2, -1)]
    groups = (TC - 2) // GROUP

    def above(p, j):
        return either(r, odd_ref[p, j].astype(F32), even_ref[p, j].astype(F32), 2 * VID)

    def below(p, j):
        return either(r, even_ref[p, j].astype(F32), odd_ref[p, j].astype(F32), 2 * VID)

    def left(i, a):
        return either(c, so_ref[i, a].astype(F32), se_ref[i, a].astype(F32), 2 * VID)

    def right(i, a):
        return either(c, se_ref[i, a].astype(F32), so_ref[i, a].astype(F32), 2 * VID)

    def sends(g):
        at = pl.ds(g * 2 * GROUP, 2 * GROUP)
        return pltpu.make_async_copy(buf.at[:, at], o_ref.at[:, at], sem.at[g])

    def put(j, rows):
        v = jnp.swapaxes(rows, 0, 1)
        for b in range(2):
            buf[:, 2 * j + b] = v[VID * b : VID * (b + 1)]

    def rows_of(j, k):
        return u_ref[k, j]

    def inner(j):
        rows = []
        for p in range(16):
            v = rows_of(j, p)
            if p < 2:
                v = (v.astype(F32) * up[p] + above(p, j + 1) * (1.0 - up[p])).astype(BF)
            elif p > 13:
                w = down[p - 14]
                v = (v.astype(F32) * (1.0 - w) + below(p - 14, j + 1) * w).astype(BF)
            rows.append(v[None])
        put(j, jnp.concatenate(rows, axis=0))

    def outer(j, side, slot, w):
        first = lax.broadcasted_iota(jnp.int32, (2 * VID, 1), 0) < VID
        w = jnp.where(first, w[0], w[1])

        def across(own, other):
            return own.astype(F32) * (1.0 - w) + other.astype(F32) * w

        rows = []
        for p in range(16):
            v = across(rows_of(j, p), side(1 + p // 2, p % 2))
            if p < 2:
                v = v * up[p] + across(above(p, j + 1), above(p, slot)) * (1.0 - up[p])
            elif p > 13:
                k = down[p - 14]
                v = v * (1.0 - k) + across(below(p - 14, j + 1), below(p - 14, slot)) * k
            rows.append(v.astype(BF)[None])
        put(j, jnp.concatenate(rows, axis=0))

    outer(0, left, 0, [1.0 - ramp(c, cr_ref, COLS, x) for x in (0, 1)])
    for j in range(1, GROUP):
        inner(j)
    sends(0).start()

    def step(g, carry):
        for j in range(GROUP):
            inner(g * GROUP + j)
        sends(g).start()
        return carry

    lax.fori_loop(1, groups - 1, step, 0)
    for j in range(TC - 2 - GROUP, TC - 3):
        inner(j)
    outer(TC - 3, right, TC - 1, [ramp(c + 1, cr_ref, COLS, x) for x in (-2, -1)])
    sends(groups - 1).start()
    for g in range(groups):
        sends(g).wait()


def lower(pos, row_ramp, col_ramp, u, fl, fr, even, odd):
    out = jax.ShapeDtypeStruct((VID, 2 * (TC - 2), 16, 2 * U), BF)
    return call(
        lower_body,
        "lower",
        out,
        (pos, row_ramp, col_ramp, u, fl, fr, even, odd),
        1 << 20,
        scratch=[
            pltpu.VMEM((VID, 2 * (TC - 2), 16, 2 * U), BF),
            pltpu.SemaphoreType.DMA(((TC - 2) // GROUP,)),
        ],
        out_specs=pl.BlockSpec(memory_space=pltpu.HBM),
        smem=3,
    )


def per_device(
    latent_tokens,
    cache_latent,
    cache_middle,
    entry_weight,
    time_weight,
    up_weight,
    norm_gain,
    row_ramp,
    col_ramp,
):
    row_pos = lax.axis_index("rows")
    col_pos = lax.axis_index("cols")
    tok = jnp.transpose(latent_tokens, (0, 2, 1))
    first, last = tok[:, :, :52], tok[:, :, 156:]
    even = row_pos % 2 == 0
    by_odd = swap(jnp.where(even, first, last), "rows", 1)
    by_even = swap(jnp.where(even, last, first), "rows", 0)
    cache = jnp.transpose(cache_latent, (0, 1, 2, 4, 3))
    cm = jnp.transpose(cache_middle, (2, 3, 0, 1, 4)).reshape(TR * TC * VID, 2 * C)
    wt = time_weight.reshape(3 * C, 2 * C)
    ut = jnp.transpose(up_weight, (0, 1, 3, 2))
    gain = norm_gain.reshape(1, U)
    pos = jnp.stack([row_pos, col_pos]).astype(jnp.int32)
    w = fold(ut)
    x, we, dl, dr, side_even, side_odd = edge(pos, tok, by_even, by_odd, cache, entry_weight, cm, wt, w, gain)
    side_even = swap(side_even, "cols", 0)
    side_odd = swap(side_odd, "cols", 1)
    rows = ends(x, we, cm, wt, dl, dr)
    to_even, to_odd = join(pos, *strips(rows, w, gain), side_even, side_odd)
    by_odd = swap(to_odd, "rows", 1)
    by_even = swap(to_even, "rows", 0)
    u = upper((x, we, cm, wt, dl, dr, *rows), w, gain, to_even)
    out = lower(pos, row_ramp, col_ramp, u, side_even, side_odd, by_even, by_odd)
    return jnp.transpose(out, (0, 2, 1, 3))


def solution(mesh):
    in_specs = (
        P(None, "rows", None),
        P(None, None, "rows", "cols", None),
        P(None, None, "rows", "cols", None),
        P(),
        P(),
        P(),
        P(),
        P(),
        P(),
    )
    out_specs = P(None, "rows", "cols", None)
    return jax.shard_map(
        per_device, mesh=mesh, in_specs=in_specs, out_specs=out_specs, check_vma=False
    )
```

```python
import functools

import jax
import jax.numpy as jnp
from jax import lax
from jax.experimental import pallas as pl
from jax.experimental.pallas import tpu as pltpu
from jax.sharding import PartitionSpec as P

EPSILON = 1e-06
BF = jnp.bfloat16
F32 = jnp.float32
VID, C, U = 8, 384, 192
TR, TC = 10, 28
ROWS, COLS = 32, 4
NT = (((1,), (1,)), ((), ()))


def swap(value, axis, first):
    size = lax.axis_size(axis)
    pairs = [(i, i + 1) for i in range(first, size - 1, 2)]
    return lax.ppermute(value, axis, pairs + [(j, i) for i, j in pairs])


def either(pos, even, odd, rows):
    return jnp.where(jnp.full((rows, 1), pos % 2, jnp.int32) == 0, even, odd)


VM = pl.BlockSpec(memory_space=pltpu.VMEM)
LIMIT = pltpu.CompilerParams(vmem_limit_bytes=24 << 20)


def held(value):
    return pltpu.with_memory_space_constraint(value, pltpu.VMEM)


def call(body, name, outs, args, flops, scratch=(), out_specs=None, smem=0):
    specs = [pl.BlockSpec(memory_space=pltpu.SMEM)] * smem + [VM] * (len(args) - smem)
    args = list(args[:smem]) + [held(v) for v in args[smem:]]
    return pl.pallas_call(
        body,
        in_specs=specs,
        out_specs=jax.tree.map(lambda _: VM, outs) if out_specs is None else out_specs,
        out_shape=outs,
        scratch_shapes=list(scratch),
        compiler_params=LIMIT,
        cost_estimate=pl.CostEstimate(flops=flops, bytes_accessed=1 << 16, transcendentals=0),
        name=name,
    )(*args)


WIDE = (TC + 2) * VID
PITCH = 56


def gather_body(row, col, tok_ref, even_ref, odd_ref, cache_ref, x_ref, t_ref, lat_ref, old_ref):
    for ref in (lat_ref, old_ref):
        for e in (0, TR + 1):
            ref[e * WIDE : (e + 1) * WIDE, :] = jnp.zeros((WIDE, 128), F32)
        for e in range(1, TR + 1):
            for u in (0, TC + 1):
                at = e * WIDE + u * VID
                ref[at : at + VID, :] = jnp.zeros((VID, 128), F32)
    t_ref[...] = jnp.zeros(t_ref.shape, F32)
    for v in range(VID):
        own = jnp.transpose(tok_ref[v].astype(F32))
        by_even, by_odd = even_ref[v].astype(F32), odd_ref[v].astype(F32)
        rows = [jnp.transpose(either(row, by_odd, by_even, 64))]
        rows += [own[52 * i : 52 * (i + 1)] for i in range(4)]
        rows += [jnp.transpose(either(row, by_even, by_odd, 64))]
        for i in range(6):
            t_ref[v % 2, pl.ds(i * PITCH + 1, 52), 0:64] = rows[i]
        for i in range(6):
            near = t_ref[v % 2, pl.ds(i * PITCH + 13 * col, 15), :]
            for q in range(2):
                e = 2 * i + q
                if e in (0, 11):
                    continue
                for k in range(2):
                    part = pltpu.roll(near, (32 - (2 * q + k) * 16) % 128, 1)
                    part = part[1:15] if k == 0 else part[0:14]
                    first = 2 if k == 0 else 1
                    lat_ref[pl.ds((e * (TC + 2) + first) * VID + v, 14, stride=2 * VID), :] = part
        for t in range(TR):
            both = jnp.concatenate([cache_ref[v, 0, t], cache_ref[v, 1, t]], axis=0).astype(F32)
            both = jnp.concatenate([both, jnp.zeros((96, TC), F32)], axis=0)
            old_ref[pl.ds(((t + 1) * (TC + 2) + 1) * VID + v, TC, stride=VID), :] = jnp.transpose(both)
    lane = lax.broadcasted_iota(jnp.int32, (1, 128), 1)
    x_ref[...] = jnp.where(lane < 32, old_ref[...], jnp.where(lane < 48, lat_ref[...], 0.0)).astype(BF)


def mixed(x_ref, we_ref, cm_ref, wt_ref, areas):
    taps, olds, sizes = [], [], []
    for r0, nr, c0, nc in areas:
        for t in range(r0, r0 + nr):
            wide = (nc + 2) * VID
            at = [(t + k) * WIDE + c0 * VID for k in range(3)]
            taps.append(jnp.concatenate([x_ref[p : p + wide, 0:48] for p in at], axis=1))
            p = (t * TC + c0) * VID
            olds.append(cm_ref[p : p + nc * VID, :])
            sizes.append(nc)
    part = jnp.dot(jnp.concatenate(taps, axis=0), we_ref[...], preferred_element_type=F32)
    part = part.reshape(-1, VID, 3 * C)
    entry, at = [], 0
    for nc in sizes:
        three = [part[at + k : at + k + nc, :, k * C : (k + 1) * C] for k in range(3)]
        entry.append(three[0] + three[1] + three[2])
        at += nc + 2
    cells = sum(sizes)
    entry = jnp.concatenate(entry, axis=0).reshape(cells * VID, C).astype(BF)
    stacked = jnp.concatenate([jnp.concatenate(olds, axis=0), entry], axis=1)
    out = jnp.dot(stacked, wt_ref[...], preferred_element_type=F32).reshape(cells, 1, VID, 2 * C)
    out = jnp.concatenate([out[..., :C], out[..., C:]], axis=1)
    return out.reshape(cells, 2 * VID, C).astype(BF)


def edge_body(
    pos_ref,
    tok_ref,
    before_ref,
    after_ref,
    cache_ref,
    ew_ref,
    cm_ref,
    wt_ref,
    ut_ref,
    gain_ref,
    x_ref,
    we_ref,
    dl_ref,
    dr_ref,
    even_ref,
    odd_ref,
    w_ref,
    t_ref,
    lat_ref,
    old_ref,
    sl_ref,
    sr_ref,
):
    fold_body(ut_ref, w_ref)
    dl_ref[...] = jnp.zeros(dl_ref.shape, BF)
    dr_ref[...] = jnp.zeros(dr_ref.shape, BF)
    for f in range(3):
        for kr in range(3):
            for kc in range(3):
                at = (kr * 3 + f) * 16
                we_ref[at : at + 16, kc * C : (kc + 1) * C] = ew_ref[f, kr, kc]
    gather_body(pos_ref[0], pos_ref[1], tok_ref, before_ref, after_ref, cache_ref, x_ref, t_ref, lat_ref, old_ref)
    d = mixed(x_ref, we_ref, cm_ref, wt_ref, ((0, TR, 0, 2), (0, TR, TC - 2, 2)))
    dl_ref[1 : TR + 1, 1:3] = d[: 2 * TR].reshape(TR, 2, 2 * VID, C)
    dr_ref[1 : TR + 1, 0:2] = d[2 * TR :].reshape(TR, 2, 2 * VID, C)
    sl_ref[...] = steps_right(dl_ref[...])
    sr_ref[...] = steps_right(dr_ref[...])
    gain = half_gain(gain_ref)
    for a in range(2):
        v = both(w_ref, gain, ((dl_ref, sl_ref, 0, TR, 0, 1), (dr_ref, sr_ref, 0, TR, 0, 1)), a)
        even_ref[:, a] = either(pos_ref[1], v[TR:].astype(F32), v[:TR].astype(F32), 2 * VID).astype(BF)
        odd_ref[:, a] = either(pos_ref[1], v[:TR].astype(F32), v[TR:].astype(F32), 2 * VID).astype(BF)


def edge(pos, tok, before, after, cache, ew, cm, wt, ut, gain):
    part = pltpu.VMEM((TR + 2, 3, 2 * VID, C), BF)
    side = jax.ShapeDtypeStruct((TR, 2, 2 * VID, 2 * U), BF)
    outs = (pltpu.VMEM((12 * WIDE, 128), BF), pltpu.VMEM((144, 3 * C), BF), part, part, side, side)
    outs += (pltpu.VMEM((2, 3, 256, 2 * C), BF),)
    return call(
        edge_body,
        "edge",
        outs,
        (pos, tok, before, after, cache, ew, cm, wt, ut, gain),
        2 * 40000 * 65536,
        scratch=[
            pltpu.VMEM((2, 6 * PITCH + 8, 128), F32),
            pltpu.VMEM((12 * WIDE, 128), F32),
            pltpu.VMEM((12 * WIDE, 128), F32),
            pltpu.VMEM((TR + 2, 2, 2 * VID, C), BF),
            pltpu.VMEM((TR + 2, 2, 2 * VID, C), BF),
        ],
        smem=1,
    )


def ends_body(x_ref, we_ref, cm_ref, wt_ref, dl_ref, dr_ref, td_ref, ts_ref, ld_ref, ls_ref):
    n = TC - 4
    for d_ref, s_ref, first, line, row in ((td_ref, ts_ref, 0, 0, 0), (ld_ref, ls_ref, TR - 1, 2, TR - 2)):
        d_ref[line, 3 : n + 3] = jnp.zeros((n, 2 * VID, C), BF)
        d_ref[:, 0:3] = dl_ref[first : first + 3]
        d_ref[:, n + 3 : n + 6] = dr_ref[first : first + 3]
        d = mixed(x_ref, we_ref, cm_ref, wt_ref, ((row, 2, 2, n),))
        at = 1 if line == 0 else 0
        d_ref[at : at + 2, 3 : n + 3] = d.reshape(2, n, 2 * VID, C)
        for i in range(3):
            s_ref[i : i + 1] = steps_right(d_ref[i : i + 1])


def rest_body(x_ref, we_ref, cm_ref, wt_ref, dl_ref, dr_ref, td_ref, ts_ref, ld_ref, ls_ref, d_ref, s_ref):
    n = TC - 4
    d_ref[0:3] = td_ref[...]
    s_ref[0:3] = ts_ref[...]
    d_ref[TR - 1 : TR + 2] = ld_ref[...]
    s_ref[TR - 1 : TR + 2] = ls_ref[...]
    d_ref[3 : TR - 1, 0:3] = dl_ref[3 : TR - 1]
    d_ref[3 : TR - 1, n + 3 : n + 6] = dr_ref[3 : TR - 1]
    for row in range(2, TR - 2, 2):
        d = mixed(x_ref, we_ref, cm_ref, wt_ref, ((row, 2, 2, n),))
        d_ref[1 + row : 3 + row, 3 : n + 3] = d.reshape(2, n, 2 * VID, C)
        for i in range(1 + row, 3 + row):
            s_ref[i : i + 1] = steps_right(d_ref[i : i + 1])


def fold_body(ut_ref, w_ref):
    for a in range(2):
        for kr in range(2):
            rows = (((0,), (1, 2)), ((0, 1), (2,)))[a][kr]
            cols = [functools.reduce(jnp.add, [ut_ref[r, c].astype(F32) for r in rows]) for c in range(3)]
            for k, w in enumerate((cols[0] + cols[1] + cols[2], -cols[0], cols[2])):
                w = w.astype(BF)
                w_ref[a, k, 0:U, kr * C : (kr + 1) * C] = w
                w_ref[a, k, U:256, kr * C : (kr + 1) * C] = w[0:64]


def steps_right(value):
    n = value.shape[1]
    return (value[:, 1:].astype(F32) - value[:, : n - 1].astype(F32)).astype(BF)


def activate(res, gain):
    cells = res.shape[0] // (2 * VID)
    res = res.reshape(cells, 2, VID, 256)
    one = res[:, 0].reshape(cells * VID, 256)
    two = res[:, 1].reshape(cells * VID, 256)
    low = lax.broadcasted_iota(jnp.int32, (1, 128), 1) < 64
    o0 = one[:, :128]
    o1 = jnp.where(low, one[:, 128:], two[:, 128:])
    o2 = jnp.where(low, two[:, 128:], two[:, :128])
    q1 = o1 * o1
    s0 = jnp.sum(o0 * o0 + jnp.where(low, q1, 0.0), axis=1, keepdims=True)
    s1 = jnp.sum(o2 * o2 + jnp.where(low, 0.0, q1), axis=1, keepdims=True)
    r0 = lax.rsqrt(s0 * (1.0 / U) + EPSILON)
    r1 = lax.rsqrt(s1 * (1.0 / U) + EPSILON)
    outs = []
    for k, (o, r) in enumerate(((o0, r0), (o1, jnp.where(low, r0, r1)), (o2, r1))):
        h = o * r * gain[:, 128 * k : 128 * (k + 1)]
        outs.append((h + h * jnp.tanh(h)).reshape(cells, 1, VID, 128))
    return outs


def both(w_ref, gain, areas, a):
    def pick(which, shift):
        parts = []
        for area in areas:
            ref, (i0, ni, j0, nj) = area[which], area[2:]
            taps = [
                ref[i0 + a + kr : i0 + a + kr + ni, j0 + shift : j0 + shift + nj].reshape(ni * nj * 2 * VID, C)
                for kr in range(2)
            ]
            parts.append(jnp.concatenate(taps, axis=1))
        return jnp.concatenate(parts, axis=0) if len(parts) > 1 else parts[0]

    def times(lhs, k):
        return lax.dot_general(lhs, w_ref[a, k], NT, preferred_element_type=F32)

    n = sum(area[3] * area[5] for area in areas)
    shared = times(pick(0, 1), 0)
    sides = [activate(shared + times(pick(1, b), 1 + b), gain) for b in range(2)]
    outs = [jnp.concatenate([u, v], axis=1).reshape(n, 2 * VID, 128).astype(BF) for u, v in zip(*sides)]
    outs[2] = jnp.concatenate([outs[2][:, :, 64:], outs[2][:, :, :64]], axis=2)
    return jnp.concatenate(outs, axis=2)


def half_gain(gain_ref):
    g = gain_ref[...] * 0.5
    return jnp.concatenate([g, g[:, :64], g[:, 128:], g[:, 64:128]], axis=1)


def strips_body(td_ref, ts_ref, ld_ref, ls_ref, w_ref, gain_ref, top_ref, low_ref):
    gain = half_gain(gain_ref)
    n = TC - 2
    for a in range(2):
        for d_ref, s_ref, ref in ((td_ref, ts_ref, top_ref), (ld_ref, ls_ref, low_ref)):
            ref[a] = both(w_ref, gain, ((d_ref, s_ref, 0, 1, 1, n),), a)


def margins_body(*refs):
    (w_ref, gain_ref), rows, tops = refs[6:8], refs[8:12], refs[12:]
    ends_body(*refs[:6], *rows)
    strips_body(*rows, w_ref, gain_ref, *tops)


def margins(x, we, cm, wt, dl, dr, w, gain):
    part = pltpu.VMEM((3, TC + 2, 2 * VID, C), BF)
    step = pltpu.VMEM((3, TC + 1, 2 * VID, C), BF)
    strip = pltpu.VMEM((2, TC - 2, 2 * VID, 2 * U), BF)
    args = (x, we, cm, wt, dl, dr, w, gain)
    return call(margins_body, "margins", (part, step, part, step, strip, strip), args, 2 * 33000 * 65536)


def join_body(pos_ref, t_ref, l_ref, se_ref, so_ref, even_ref, odd_ref):
    n = TC - 2
    even = pos_ref[0] % 2 == 0

    def put(ref, own_ref, i):
        ref[:, 1 : n + 1] = own_ref[...]
        for a in range(2):
            by_even, by_odd = se_ref[i, a].astype(F32), so_ref[i, a].astype(F32)
            ref[a, 0] = either(pos_ref[1], by_odd, by_even, 2 * VID).astype(BF)
            ref[a, n + 1] = either(pos_ref[1], by_even, by_odd, 2 * VID).astype(BF)

    @pl.when(even)
    def _():
        put(even_ref, l_ref, TR - 1)
        put(odd_ref, t_ref, 0)

    @pl.when(jnp.logical_not(even))
    def _():
        put(even_ref, t_ref, 0)
        put(odd_ref, l_ref, TR - 1)


def join(pos, t, l, fl, fr):
    strip = jax.ShapeDtypeStruct((2, TC, 2 * VID, 2 * U), BF)
    return call(join_body, "join", (strip, strip), (pos, t, l, fl, fr), 1 << 20, smem=1)


def upper_body(*refs):
    parts, (w_ref, gain_ref, _, o_ref, d_ref, s_ref) = refs[:10], refs[10:]
    rest_body(*parts, d_ref, s_ref)
    gain = half_gain(gain_ref)
    for i in range(TR - 2):
        for a in range(2):
            o_ref[2 * i + a] = both(w_ref, gain, ((d_ref, s_ref, i + 1, 1, 1, TC - 2),), a)


def upper(parts, w, gain, after):
    return call(
        upper_body,
        "upper",
        pltpu.VMEM((2 * (TR - 2), TC - 2, 2 * VID, 2 * U), BF),
        (*parts, w, gain, after),
        2 * (27000 + (TR - 2) * 416 * 18) * 65536,
        scratch=[
            pltpu.VMEM((TR + 2, TC + 2, 2 * VID, C), BF),
            pltpu.VMEM((TR + 2, TC + 1, 2 * VID, C), BF),
        ],
    )


def ramp(pos, table_ref, amount, place):
    step = table_ref[jnp.clip(pos, 1, amount - 1)].astype(F32)
    sloped = jnp.clip(jnp.full((1, 1), place + 0.5, F32) / jnp.full((1, 1), step, F32) + 0.5, 0.0, 1.0)
    return jnp.where(pos <= 0, 1.0, jnp.where(pos >= amount, 0.0, sloped))


GROUP = 2


def lower_body(pos_ref, rr_ref, cr_ref, u_ref, se_ref, so_ref, even_ref, odd_ref, o_ref, buf, sem):
    r, c = pos_ref[0], pos_ref[1]
    up = [ramp(r, rr_ref, ROWS, p) for p in (0, 1)]
    down = [ramp(r + 1, rr_ref, ROWS, p) for p in (-2, -1)]
    groups = (TC - 2) // GROUP

    def above(p, j):
        return either(r, odd_ref[p, j].astype(F32), even_ref[p, j].astype(F32), 2 * VID)

    def below(p, j):
        return either(r, even_ref[p, j].astype(F32), odd_ref[p, j].astype(F32), 2 * VID)

    def left(i, a):
        return either(c, so_ref[i, a].astype(F32), se_ref[i, a].astype(F32), 2 * VID)

    def right(i, a):
        return either(c, se_ref[i, a].astype(F32), so_ref[i, a].astype(F32), 2 * VID)

    def sends(g):
        at = pl.ds(g * 2 * GROUP, 2 * GROUP)
        return pltpu.make_async_copy(buf.at[:, at], o_ref.at[:, at], sem.at[g])

    def put(j, rows):
        v = jnp.swapaxes(rows, 0, 1)
        for b in range(2):
            buf[:, 2 * j + b] = v[VID * b : VID * (b + 1)]

    def rows_of(j, k):
        return u_ref[k, j]

    def inner(j):
        rows = []
        for p in range(16):
            v = rows_of(j, p)
            if p < 2:
                v = (v.astype(F32) * up[p] + above(p, j + 1) * (1.0 - up[p])).astype(BF)
            elif p > 13:
                w = down[p - 14]
                v = (v.astype(F32) * (1.0 - w) + below(p - 14, j + 1) * w).astype(BF)
            rows.append(v[None])
        put(j, jnp.concatenate(rows, axis=0))

    def outer(j, side, slot, w):
        first = lax.broadcasted_iota(jnp.int32, (2 * VID, 1), 0) < VID
        w = jnp.where(first, w[0], w[1])

        def across(own, other):
            return own.astype(F32) * (1.0 - w) + other.astype(F32) * w

        rows = []
        for p in range(16):
            v = across(rows_of(j, p), side(1 + p // 2, p % 2))
            if p < 2:
                v = v * up[p] + across(above(p, j + 1), above(p, slot)) * (1.0 - up[p])
            elif p > 13:
                k = down[p - 14]
                v = v * (1.0 - k) + across(below(p - 14, j + 1), below(p - 14, slot)) * k
            rows.append(v.astype(BF)[None])
        put(j, jnp.concatenate(rows, axis=0))

    outer(0, left, 0, [1.0 - ramp(c, cr_ref, COLS, x) for x in (0, 1)])
    for j in range(1, GROUP):
        inner(j)
    sends(0).start()

    def step(g, carry):
        for j in range(GROUP):
            inner(g * GROUP + j)
        sends(g).start()
        return carry

    lax.fori_loop(1, groups - 1, step, 0)
    for j in range(TC - 2 - GROUP, TC - 3):
        inner(j)
    outer(TC - 3, right, TC - 1, [ramp(c + 1, cr_ref, COLS, x) for x in (-2, -1)])
    sends(groups - 1).start()
    for g in range(groups):
        sends(g).wait()


def lower(pos, row_ramp, col_ramp, u, fl, fr, even, odd):
    out = jax.ShapeDtypeStruct((VID, 2 * (TC - 2), 16, 2 * U), BF)
    return call(
        lower_body,
        "lower",
        out,
        (pos, row_ramp, col_ramp, u, fl, fr, even, odd),
        1 << 20,
        scratch=[
            pltpu.VMEM((VID, 2 * (TC - 2), 16, 2 * U), BF),
            pltpu.SemaphoreType.DMA(((TC - 2) // GROUP,)),
        ],
        out_specs=pl.BlockSpec(memory_space=pltpu.HBM),
        smem=3,
    )


def per_device(
    latent_tokens,
    cache_latent,
    cache_middle,
    entry_weight,
    time_weight,
    up_weight,
    norm_gain,
    row_ramp,
    col_ramp,
):
    row_pos = lax.axis_index("rows")
    col_pos = lax.axis_index("cols")
    tok = jnp.transpose(latent_tokens, (0, 2, 1))
    first, last = tok[:, :, :52], tok[:, :, 156:]
    even = row_pos % 2 == 0
    by_odd = swap(jnp.where(even, first, last), "rows", 1)
    by_even = swap(jnp.where(even, last, first), "rows", 0)
    cache = jnp.transpose(cache_latent, (0, 1, 2, 4, 3))
    cm = jnp.transpose(cache_middle, (2, 3, 0, 1, 4)).reshape(TR * TC * VID, 2 * C)
    wt = time_weight.reshape(3 * C, 2 * C)
    ut = jnp.transpose(up_weight, (0, 1, 3, 2))
    gain = norm_gain.reshape(1, U)
    pos = jnp.stack([row_pos, col_pos]).astype(jnp.int32)
    x, we, dl, dr, side_even, side_odd, w = edge(pos, tok, by_even, by_odd, cache, entry_weight, cm, wt, ut, gain)
    side_even = swap(side_even, "cols", 0)
    side_odd = swap(side_odd, "cols", 1)
    *rows, top, low = margins(x, we, cm, wt, dl, dr, w, gain)
    to_even, to_odd = join(pos, top, low, side_even, side_odd)
    by_odd = swap(to_odd, "rows", 1)
    by_even = swap(to_even, "rows", 0)
    u = upper((x, we, cm, wt, dl, dr, *rows), w, gain, to_even)
    out = lower(pos, row_ramp, col_ramp, u, side_even, side_odd, by_even, by_odd)
    return jnp.transpose(out, (0, 2, 1, 3))


def solution(mesh):
    in_specs = (
        P(None, "rows", None),
        P(None, None, "rows", "cols", None),
        P(None, None, "rows", "cols", None),
        P(),
        P(),
        P(),
        P(),
        P(),
        P(),
    )
    out_specs = P(None, "rows", "cols", None)
    return jax.shard_map(
        per_device, mesh=mesh, in_specs=in_specs, out_specs=out_specs, check_vma=False
    )
```
